256 devices in a mesh: inp: 128 (over z_lo, x, y, core), tm: 2 (over z_hi).
Axes of the slice: x: 4, y: 4, z: 8 (z_hi: 2, z_lo: 4; z = z_hi * 4 + z_lo), core: 2. Of those that a mesh axis runs over, the one named last changes fastest.
Arguments:
- samples: bfloat16 [768, 128, 3072], P('inp', 'tm'), may hold values from -6 to 6
Outputs:
- visibilities: float32 [512, 2, 768, 768], P(('inp', 'tm'))
The draws below stay inside these ranges and needn't reach their ends.
All inputs are finite; a program needn't handle non-finite values.
Results may differ from the reference program's by a relative error of at most 0.0095.
Values may be sent and summed in bfloat16 or wider, within the bound.
A program may use at most 128 MiB of HBM per device.

```python
import jax
import jax.numpy as jnp
from jax import lax

FRAME = 3072
TAPS = 4
CH = 512
FIRST = 256
INPUTS = 768
SPECTRA = 128


def block_scale(rng, extent, split, low, largest):
    gain, own = 1.0, jax.random.fold_in(rng, 6)
    for dim, blocks in split:
        steps = jnp.exp(jax.random.uniform(jax.random.fold_in(own, dim), (blocks,), jnp.float32, low / len(split), largest / len(split)))
        gain = gain * jnp.repeat(steps, extent[dim] // blocks).reshape([-1 if axis == dim else 1 for axis in range(len(extent))])
    return gain


def scatter_about(stream_key, dims, scale, most, pieces=(), kind=jnp.bfloat16):
    values = scale * jax.random.normal(stream_key, dims, jnp.float32)
    if pieces:
        values = values * block_scale(stream_key, dims, pieces, -0.22, 0.18)
    return jnp.clip(values, -most, most).astype(kind)


def setup_inputs(seed: int = 0) -> dict:
    splits = jax.random.split(jax.random.key(seed), 2)
    samples = scatter_about(splits[0], (INPUTS, SPECTRA, FRAME), 1.0, 6.0, ((0, 128), (1, 2)))
    return dict(samples=samples)


def pfb_weights():
    total = TAPS * FRAME
    place = jnp.arange(total, dtype=jnp.float32)
    centred = (place - (total - 1) / 2.0) / FRAME
    taper = 0.5 - 0.5 * jnp.cos(2.0 * jnp.pi * (place + 0.5) / total)
    shape_vals = jnp.sinc(centred) * taper
    norm_value = jnp.sqrt(jnp.sum(shape_vals * shape_vals) / FRAME)
    return (shape_vals / norm_value).reshape(TAPS, FRAME)

def dft_table():
    sample_idx = jnp.arange(FRAME, dtype=jnp.int32)
    chan_idx = FIRST + jnp.arange(CH, dtype=jnp.int32)
    phase_idx = sample_idx[:, None] * chan_idx[None, :] % FRAME
    angle = 2.0 * jnp.pi * phase_idx.astype(jnp.float32) / FRAME
    scaling = jnp.sqrt(2.0 / FRAME)
    return (jnp.concatenate([jnp.cos(angle), -jnp.sin(angle)], axis=1) * scaling).astype(jnp.bfloat16)

def reference(samples):
    total_spec = samples.shape[1]
    weights = pfb_weights()
    table = dft_table()

    def one_input(signal):
        extended = jnp.concatenate([jnp.zeros((TAPS - 1, FRAME), jnp.float32), signal.astype(jnp.float32)], axis=0)
        filtered = weights[0] * extended[0:total_spec]
        for tap_index in range(1, TAPS):
            filtered = filtered + weights[tap_index] * extended[tap_index:tap_index + total_spec]
        return jnp.dot(filtered.astype(jnp.bfloat16), table, preferred_element_type=jnp.float32).astype(jnp.bfloat16)
    spectra = lax.map(one_input, samples)
    spectra = spectra.reshape(INPUTS, total_spec, 2, CH).transpose(3, 2, 0, 1)

    def one_channel(block):
        real_part = jnp.dot(block[0], block[0].T, preferred_element_type=jnp.float32) + jnp.dot(block[1], block[1].T, preferred_element_type=jnp.float32)
        imag_part = jnp.dot(block[1], block[0].T, preferred_element_type=jnp.float32) - jnp.dot(block[0], block[1].T, preferred_element_type=jnp.float32)
        return jnp.stack([real_part, imag_part], axis=0)
    visibilities = lax.map(one_channel, spectra)
    return visibilities * (1.0 / total_spec)
```

```python
import numpy as np
import jax
import jax.numpy as jnp
import ml_dtypes
from jax import lax
from jax.experimental import pallas as pl
from jax.experimental.pallas import tpu as pltpu
from jax.sharding import PartitionSpec as P

FRAME = 3072
TAPS = 4
CH = 512
FIRST = 256
MESH = pl.DeviceIdType.MESH
F32 = jnp.float32
BF16 = jnp.bfloat16
LANE_TILES = FRAME // 128
NT = (((1,), (1,)), ((), ()))


def pfb_weights():
    total = TAPS * FRAME
    place = np.arange(total, dtype=np.float64)
    centred = (place - (total - 1) / 2.0) / FRAME
    taper = 0.5 - 0.5 * np.cos(2.0 * np.pi * (place + 0.5) / total)
    vals = np.sinc(centred) * taper
    return (vals / np.sqrt(np.sum(vals * vals) / FRAME)).reshape(TAPS, FRAME).astype(np.float32)


def dft_rows():
    xd, zd, yd, cd, ch2 = np.meshgrid(
        np.arange(4), np.arange(8), np.arange(4), np.arange(2), np.arange(2), indexing="ij"
    )
    chan = (zd % 4) * 128 + xd * 32 + yd * 8 + cd * 4 + (zd // 4) * 2 + ch2
    chan = chan.reshape(4, 128)
    phase = ((chan[:, :, None] + FIRST) * np.arange(FRAME)[None, None, :]) % FRAME
    angle = 2.0 * np.pi * np.arange(FRAME) / FRAME
    scale = np.sqrt(2.0 / FRAME)
    cos = (np.cos(angle) * scale).astype(ml_dtypes.bfloat16)
    sin = (-np.sin(angle) * scale).astype(ml_dtypes.bfloat16)
    return np.concatenate([cos[phase], sin[phase]], axis=1)


def shuffle(source):
    n = source.size
    out = np.zeros((n, n), ml_dtypes.bfloat16)
    out[np.arange(n), source.reshape(-1)] = 1.0
    return out


def middle_shuffle():
    place = np.arange(384).reshape(4, 6, 8, 2)
    return shuffle(place.transpose(2, 3, 0, 1))


def final_shuffle():
    place = np.arange(384).reshape(8, 2, 4, 6)
    return shuffle(place.transpose(1, 2, 0, 3))


def turn_kernel(
    samples, table, window, perm, out,
    xs, tabs, stage, tail, filt, send, mid0, mid1, pack,
    x_sem, t_sem, z_send, z_recv, p_send, p_recv,
):
    inp = lax.axis_index("inp")
    t = lax.axis_index("tm")
    zl, xyc = inp // 32, inp % 32
    x, y, core = xyc // 8, (xyc // 2) % 4, xyc % 2
    z = t * 4 + zl

    def hop(q):
        return jnp.where(q == 0, 2, jnp.where(q == 1, 1, jnp.where(q == 2, 3, 0)))

    def z_device(place):
        return ((place % 4) * 32 + xyc, place // 4)

    def p_device(xd, yc):
        return (zl * 32 + xd * 8 + yc, t)

    for i in range(6):
        pltpu.make_async_copy(samples.at[i], xs.at[i], x_sem.at[i]).start()
    for q in range(4):
        xd = (x + hop(q)) % 4
        pltpu.make_async_copy(table.at[xd], tabs.at[q], t_sem.at[q]).start()

    barrier = pltpu.get_barrier_semaphore()
    for k in range(1, 8):
        pl.semaphore_signal(barrier, inc=1, device_id=z_device((z + k) % 8), device_id_type=MESH)
    def greet(k, _):
        other = (xyc + k) % 32
        pl.semaphore_signal(barrier, inc=1, device_id=(zl * 32 + other, t), device_id_type=MESH)
        return 0
    lax.fori_loop(1, 32, greet, 0)

    stage[:, 0:8, :] = jnp.zeros((LANE_TILES, 8, 128), F32)
    stage[:, 72:80, :] = jnp.zeros((LANE_TILES, 8, 128), F32)

    def filter_input(i, _):
        pltpu.make_async_copy(samples.at[i], xs.at[i], x_sem.at[i]).wait()
        for c in range(LANE_TILES):
            stage[c, 8:72, :] = xs[i, :, c * 128 : (c + 1) * 128].astype(F32)
        for c in range(LANE_TILES):
            cols = slice(c * 128, (c + 1) * 128)
            acc = window[0:1, cols] * stage[c, 5:77, :]
            for k in range(1, TAPS):
                acc = acc + window[k : k + 1, cols] * stage[c, 5 + k : 77 + k, :]
            filt[pl.ds(pl.multiple_of(i * 64, 64), 64), cols] = acc[0:64].astype(BF16)
            tail[pl.ds(pl.multiple_of(i * 8, 8), 8), cols] = acc[64:72]
        return 0

    lax.fori_loop(0, 6, filter_input, 0)
    filt[384:432, :] = tail[...].astype(BF16)
    filt[432:512, :] = jnp.zeros((80, FRAME), BF16)

    def z_copies(q, blocks, mid, sem):
        copies = []
        for k in range(1, 8):
            place = (z + k) % 8
            rows = pl.ds(pl.multiple_of(place * 16, 16), 16)
            copies.append(
                pltpu.make_async_remote_copy(
                    send.at[q, pl.ds(0, blocks), rows, :], mid.at[q, zl], z_send.at[q], sem.at[q],
                    device_id=z_device(place), device_id_type=MESH,
                )
            )
        rows = pl.ds(pl.multiple_of(z * 16, 16), 16)
        own = pltpu.make_async_copy(send.at[q, pl.ds(0, blocks), rows, :], mid.at[q, zl], sem.at[q])
        return copies, own

    low = lax.broadcasted_iota(jnp.int32, (128, 128), 1) < 64

    def spectra(q, _):
        pltpu.make_async_copy(table.at[0], tabs.at[q], t_sem.at[q]).wait()
        prod = lax.dot_general(tabs[q], filt[...], NT, preferred_element_type=F32)
        for pair in range(3):
            re = prod[0:128, pair * 128 : (pair + 1) * 128]
            im = prod[128:256, pair * 128 : (pair + 1) * 128]
            send[q, 2 * pair] = jnp.where(low, re, pltpu.roll(im, 64, 1)).astype(BF16)
            send[q, 2 * pair + 1] = jnp.where(low, pltpu.roll(re, 64, 1), im).astype(BF16)
        re, im = prod[0:128, 384:512], prod[128:256, 384:512]
        send[q, 6] = jnp.where(low, re, pltpu.roll(im, 64, 1)).astype(BF16)

        @pl.when(q == 0)
        def _():
            pl.semaphore_wait(barrier, 38)

        @pl.when(t == 0)
        def _():
            copies, own = z_copies(q, 7, mid0, z_recv.at[0])
            for copy in copies:
                copy.start()
            own.start()

        @pl.when(t == 1)
        def _():
            copies, own = z_copies(q, 6, mid1, z_recv.at[1])
            for copy in copies:
                copy.start()
            own.start()

        return 0

    lax.fori_loop(0, 4, spectra, 0)

    lane = lax.broadcasted_iota(jnp.int32, (16, 128), 1)
    first = (lane % 64) < TAPS - 1

    def turn(q, _):
        pltpu.make_async_copy(mid0.at[q], mid0.at[q], z_recv.at[0, q]).wait()
        pltpu.make_async_copy(mid1.at[q], mid1.at[q], z_recv.at[1, q]).wait()
        later = []
        for a in range(4):
            extra = mid0[q, a, 6].astype(F32)
            for i in range(6):
                moved = extra if i == 0 else pltpu.roll(extra, 128 - 8 * i, 1)
                later.append((mid1[q, a, i].astype(F32) + jnp.where(first, moved, 0.0)).astype(BF16))
        earlier = [mid0[q, a, i] for a in range(4) for i in range(6)]
        both = jnp.concatenate([jnp.concatenate(earlier, 0), jnp.concatenate(later, 0)], 1)
        turned = jnp.dot(perm[...], both, preferred_element_type=F32).astype(BF16)
        for yc in range(8):
            for half in range(2):
                pack[q, yc, half] = turned[yc * 48 : (yc + 1) * 48, half * 128 : (half + 1) * 128]
        xd = (x + hop(q)) % 4

        def pass_on(k, _):
            yc = (xyc + k) % 8
            pltpu.make_async_remote_copy(
                pack.at[q, yc], out.at[xyc], p_send, p_recv, device_id=p_device(xd, yc), device_id_type=MESH
            ).start()
            return 0

        @pl.when(q < 3)
        def _():
            pltpu.make_async_remote_copy(
                pack.at[q, xyc % 8], out.at[xyc], p_send, p_recv,
                device_id=p_device(xd, xyc % 8), device_id_type=MESH,
            ).start()

        @pl.when(q == 3)
        def _():
            pltpu.make_async_copy(pack.at[q, xyc % 8], out.at[xyc], p_recv).start()

        lax.fori_loop(1, 8, pass_on, 0)
        return 0

    lax.fori_loop(0, 4, turn, 0)

    pltpu.make_async_copy(out, out, p_recv).wait()

    def sent(k, _):
        pltpu.make_async_copy(pack.at[0, 0], pack.at[0, 0], p_send).wait()
        return 0

    lax.fori_loop(0, 31, sent, 0)

    def z_sent(q, _):
        @pl.when(t == 0)
        def _():
            for copy in z_copies(q, 7, mid0, z_recv.at[0])[0]:
                copy.wait_send()

        @pl.when(t == 1)
        def _():
            for copy in z_copies(q, 6, mid1, z_recv.at[1])[0]:
                copy.wait_send()

        return 0

    lax.fori_loop(0, 4, z_sent, 0)


def corner_turn(samples, table, window, perm):
    dma = pltpu.SemaphoreType.DMA
    anywhere = pl.BlockSpec(memory_space=pl.ANY)
    vmem = pl.BlockSpec(memory_space=pltpu.VMEM)
    return pl.pallas_call(
        turn_kernel,
        out_shape=jax.ShapeDtypeStruct((32, 2, 48, 128), BF16),
        in_specs=[anywhere, anywhere, vmem, vmem],
        out_specs=anywhere,
        scratch_shapes=[
            pltpu.VMEM((6, 64, FRAME), BF16),
            pltpu.VMEM((4, 256, FRAME), BF16),
            pltpu.VMEM((LANE_TILES, 80, 128), F32),
            pltpu.VMEM((48, FRAME), F32),
            pltpu.VMEM((512, FRAME), BF16),
            pltpu.VMEM((4, 7, 128, 128), BF16),
            pltpu.VMEM((4, 4, 7, 16, 128), BF16),
            pltpu.VMEM((4, 4, 6, 16, 128), BF16),
            pltpu.VMEM((4, 8, 2, 48, 128), BF16),
            dma((6,)), dma((4,)), dma((4,)), dma((2, 4)), dma, dma,
        ],
        compiler_params=pltpu.CompilerParams(
            collective_id=1, has_side_effects=True, vmem_limit_bytes=48 << 20
        ),
        name="corner_turn",
    )(samples, table, window, perm)


def correlate_kernel(turned, perm, out, left, swapped, vis, sem):
    for o in range(4):
        halves = [jnp.concatenate([turned[8 * o + k, h] for k in range(8)], 0) for h in range(2)]
        rows = jnp.dot(perm[...], jnp.concatenate(halves, 1), preferred_element_type=F32)
        low = (lax.broadcasted_iota(jnp.int32, rows.shape, 1) % 128) < 64
        parts = [pltpu.roll(rows[:, h * 128 : (h + 1) * 128], 64, 1) for h in range(2)]
        other = jnp.concatenate(parts, 1)
        other = jnp.where(low, other, -other)
        rows, other = rows.astype(BF16), other.astype(BF16)
        for ch in range(2):
            for a in range(4):
                src = slice((ch * 4 + a) * 48, (ch * 4 + a + 1) * 48)
                dst = slice(a * 192 + o * 48, a * 192 + (o + 1) * 48)
                left[ch, dst] = rows[src]
                swapped[ch, dst] = other[src]
    copies = []
    for ch in range(2):
        for part, mat in enumerate((left, swapped)):
            for r in range(3):
                block = slice(r * 256, (r + 1) * 256)
                vis[ch, part, block] = lax.dot_general(
                    mat[ch, block], left[ch], NT, preferred_element_type=F32
                ) * (1.0 / 128.0)
                copy = pltpu.make_async_copy(
                    vis.at[ch, part, pl.ds(r * 256, 256)],
                    out.at[ch, part, pl.ds(r * 256, 256)],
                    sem.at[ch, part, r],
                )
                copy.start()
                copies.append(copy)
    for copy in copies:
        copy.wait()


def correlate(turned, perm):
    vmem = pl.BlockSpec(memory_space=pltpu.VMEM)
    return pl.pallas_call(
        correlate_kernel,
        out_shape=jax.ShapeDtypeStruct((2, 2, 768, 768), F32),
        in_specs=[vmem, vmem],
        out_specs=pl.BlockSpec(memory_space=pl.ANY),
        scratch_shapes=[
            pltpu.VMEM((2, 768, 256), BF16),
            pltpu.VMEM((2, 768, 256), BF16),
            pltpu.VMEM((2, 2, 768, 768), F32),
            pltpu.SemaphoreType.DMA((2, 2, 3)),
        ],
        compiler_params=pltpu.CompilerParams(vmem_limit_bytes=48 << 20),
        name="correlate",
    )(turned, perm)


def local(samples):
    turned = corner_turn(
        samples, jnp.asarray(dft_rows()), jnp.asarray(pfb_weights()), jnp.asarray(middle_shuffle())
    )
    return correlate(turned, jnp.asarray(final_shuffle()))


def solution(mesh):
    return jax.shard_map(
        local,
        mesh=mesh,
        in_specs=(P("inp", "tm", None),),
        out_specs=P(("inp", "tm"), None, None, None),
        check_vma=False,
    )
```

```python
import numpy as np
import jax
import jax.numpy as jnp
import ml_dtypes
from jax import lax
from jax.experimental import pallas as pl
from jax.experimental.pallas import tpu as pltpu
from jax.sharding import PartitionSpec as P

FRAME = 3072
TAPS = 4
CH = 512
FIRST = 256
MESH = pl.DeviceIdType.MESH
F32 = jnp.float32
BF16 = jnp.bfloat16
LANE_TILES = FRAME // 128
RING = (4, 3, 5, 2, 6, 1, 7)
NT = (((1,), (1,)), ((), ()))


def pfb_weights():
    total = TAPS * FRAME
    place = np.arange(total, dtype=np.float64)
    centred = (place - (total - 1) / 2.0) / FRAME
    taper = 0.5 - 0.5 * np.cos(2.0 * np.pi * (place + 0.5) / total)
    vals = np.sinc(centred) * taper
    return (vals / np.sqrt(np.sum(vals * vals) / FRAME)).reshape(TAPS, FRAME).astype(np.float32)


def dft_rows():
    xd, zd, yd, cd, ch2 = np.meshgrid(
        np.arange(4), np.arange(8), np.arange(4), np.arange(2), np.arange(2), indexing="ij"
    )
    chan = (zd % 4) * 128 + xd * 32 + yd * 8 + cd * 4 + (zd // 4) * 2 + ch2
    chan = chan.reshape(4, 128)
    phase = ((chan[:, :, None] + FIRST) * np.arange(FRAME)[None, None, :]) % FRAME
    angle = 2.0 * np.pi * np.arange(FRAME) / FRAME
    scale = np.sqrt(2.0 / FRAME)
    cos = (np.cos(angle) * scale).astype(ml_dtypes.bfloat16)
    sin = (-np.sin(angle) * scale).astype(ml_dtypes.bfloat16)
    return np.concatenate([cos[phase], sin[phase]], axis=1)


def shuffle(source):
    n = source.size
    out = np.zeros((n, n), ml_dtypes.bfloat16)
    out[np.arange(n), source.reshape(-1)] = 1.0
    return out


def middle_shuffle():
    place = np.arange(384).reshape(4, 6, 8, 2)
    return shuffle(place.transpose(2, 3, 0, 1))


def final_shuffle():
    place = np.arange(384).reshape(8, 2, 4, 6)
    return shuffle(place.transpose(1, 2, 0, 3))


def turn_kernel(
    samples, table, window_hbm, perm_hbm, out,
    xs, tabs, window, perm, stage, tail, filt, extras, send, mid0, mid1, pack,
    x_sem, t_sem, w_sem, z_send, z_recv, p_send, p_recv,
):
    inp = lax.axis_index("inp")
    t = lax.axis_index("tm")
    zl, xyc = inp // 32, inp % 32
    x, y, core = xyc // 8, (xyc // 2) % 4, xyc % 2
    z = t * 4 + zl

    def hop(q):
        return jnp.where(q == 0, 2, jnp.where(q == 1, 1, jnp.where(q == 2, 3, 0)))

    def z_device(place):
        return ((place % 4) * 32 + xyc, place // 4)

    def p_device(xd, yc):
        return (zl * 32 + xd * 8 + yc, t)

    for i in range(6):
        pltpu.make_async_copy(samples.at[i], xs.at[i], x_sem.at[i]).start()
    pltpu.make_async_copy(window_hbm, window, w_sem.at[0]).start()
    for q in range(4):
        xd = (x + hop(q)) % 4
        pltpu.make_async_copy(table.at[xd], tabs.at[q], t_sem.at[q]).start()

    pltpu.make_async_copy(perm_hbm, perm, w_sem.at[1]).start()

    barrier = pltpu.get_barrier_semaphore()
    for k in RING:
        pl.semaphore_signal(barrier, inc=1, device_id=z_device((z + k) % 8), device_id_type=MESH)
    def greet(k, _):
        other = (xyc + k) % 32
        pl.semaphore_signal(barrier, inc=1, device_id=(zl * 32 + other, t), device_id_type=MESH)
        return 0
    lax.fori_loop(1, 32, greet, 0)

    stage[:, 0:8, :] = jnp.zeros((LANE_TILES, 8, 128), F32)
    stage[:, 72:80, :] = jnp.zeros((LANE_TILES, 8, 128), F32)

    pltpu.make_async_copy(window_hbm, window, w_sem.at[0]).wait()

    def filter_input(i, _):
        pltpu.make_async_copy(samples.at[i], xs.at[i], x_sem.at[i]).wait()
        for c in range(LANE_TILES):
            stage[c, 8:72, :] = xs[i, :, c * 128 : (c + 1) * 128].astype(F32)
        for c in range(LANE_TILES):
            cols = slice(c * 128, (c + 1) * 128)
            acc = window[0:1, cols] * stage[c, 5:77, :]
            for k in range(1, TAPS):
                acc = acc + window[k : k + 1, cols] * stage[c, 5 + k : 77 + k, :]
            filt[pl.ds(pl.multiple_of(i * 64, 64), 64), cols] = acc[0:64].astype(BF16)
            tail[i, :, cols] = acc[64:72]
        return 0

    lax.fori_loop(0, 6, filter_input, 0)
    reach = [tail[i, 0 : TAPS - 1, :] for i in range(6)]
    filt[384:416, :] = jnp.concatenate(reach + [jnp.zeros((14, FRAME), F32)], 0).astype(BF16)
    filt[416:512, :] = jnp.zeros((96, FRAME), BF16)
    extras[...] = jnp.zeros((128, 128), F32)

    def z_copies(q, blocks, mid, sem):
        copies = []
        for k in RING:
            place = (z + k) % 8
            rows = pl.ds(pl.multiple_of(place * 16, 16), 16)
            copies.append(
                pltpu.make_async_remote_copy(
                    send.at[q, pl.ds(0, blocks), rows, :], mid.at[q, zl, pl.ds(0, blocks)], z_send.at[q], sem.at[q],
                    device_id=z_device(place), device_id_type=MESH,
                )
            )
        rows = pl.ds(pl.multiple_of(z * 16, 16), 16)
        own = pltpu.make_async_copy(send.at[q, pl.ds(0, blocks), rows, :], mid.at[q, zl, pl.ds(0, blocks)], sem.at[q])
        return copies, own

    def send_z(q, blocks, mid, sem):
        copies, own = z_copies(q, blocks, mid, sem)
        for copy in copies:
            copy.start()
        own.start()

    low = lax.broadcasted_iota(jnp.int32, (128, 128), 1) < 64

    def spectra(q, _):
        pltpu.make_async_copy(table.at[0], tabs.at[q], t_sem.at[q]).wait()
        prod = lax.dot_general(tabs[q], filt[...], NT, preferred_element_type=F32)
        for pair in range(3):
            re = prod[0:128, pair * 128 : (pair + 1) * 128]
            im = prod[128:256, pair * 128 : (pair + 1) * 128]
            send[q, 2 * pair] = jnp.where(low, re, pltpu.roll(im, 64, 1)).astype(BF16)
            send[q, 2 * pair + 1] = jnp.where(low, pltpu.roll(re, 64, 1), im).astype(BF16)
        re, im = prod[0:128, 384:512], prod[128:256, 384:512]

        @pl.when(q == 0)
        def _():
            send[0, 6] = (re + pltpu.roll(im, 20, 1)).astype(BF16)
            pl.semaphore_wait(barrier, 38)

        @pl.when(q > 0)
        def _():
            slot = (q - 1) * 40
            extras[...] += pltpu.roll(re, slot, 1) + pltpu.roll(im, slot + 20, 1)

        @pl.when((t == 0) & (q == 0))
        def _():
            send_z(q, 7, mid0, z_recv.at[0])

        @pl.when(t == 1)
        def _():
            send_z(q, 6, mid1, z_recv.at[1])

        return 0

    lax.fori_loop(0, 4, spectra, 0)

    @pl.when(t == 0)
    def _():
        send[1, 6] = extras[...].astype(BF16)
        send_z(1, 7, mid0, z_recv.at[0])
        for q in range(2, 4):
            send_z(q, 6, mid0, z_recv.at[0])

    lane = lax.broadcasted_iota(jnp.int32, (16, 128), 1)
    first = lane < TAPS - 1
    second = (lane >= 64) & (lane < 64 + TAPS - 1)
    pltpu.make_async_copy(perm_hbm, perm, w_sem.at[1]).wait()

    def turn(q, _):
        @pl.when(q < 2)
        def _():
            pltpu.make_async_copy(mid0.at[q], mid0.at[q], z_recv.at[0, q]).wait()

        @pl.when(q >= 2)
        def _():
            pltpu.make_async_copy(mid1.at[q], mid1.at[q], z_recv.at[0, q]).wait()

        pltpu.make_async_copy(mid1.at[q], mid1.at[q], z_recv.at[1, q]).wait()
        later = []
        slot = jnp.maximum(q - 1, 0) * 40
        for a in range(4):
            extra = mid0[jnp.minimum(q, 1), a, 6].astype(F32)
            for i in range(6):
                re = pltpu.roll(extra, (128 - 3 * i - slot) % 128, 1)
                im = pltpu.roll(extra, (172 - 3 * i - slot) % 128, 1)
                added = jnp.where(first, re, jnp.where(second, im, 0.0))
                later.append((mid1[q, a, i].astype(F32) + added).astype(BF16))
        earlier = [mid0[q, a, i] for a in range(4) for i in range(6)]
        both = jnp.concatenate([jnp.concatenate(earlier, 0), jnp.concatenate(later, 0)], 1)
        turned = jnp.dot(perm[...], both, preferred_element_type=F32).astype(BF16)
        for yc in range(8):
            for half in range(2):
                pack[q, yc, half] = turned[yc * 48 : (yc + 1) * 48, half * 128 : (half + 1) * 128]
        xd = (x + hop(q)) % 4

        def pass_on(k, _):
            yc = (xyc + k) % 8
            pltpu.make_async_remote_copy(
                pack.at[q, yc], out.at[xyc], p_send, p_recv, device_id=p_device(xd, yc), device_id_type=MESH
            ).start()
            return 0

        @pl.when(q < 3)
        def _():
            pltpu.make_async_remote_copy(
                pack.at[q, xyc % 8], out.at[xyc], p_send, p_recv,
                device_id=p_device(xd, xyc % 8), device_id_type=MESH,
            ).start()

        @pl.when(q == 3)
        def _():
            pltpu.make_async_copy(pack.at[q, xyc % 8], out.at[xyc], p_recv).start()

        lax.fori_loop(1, 8, pass_on, 0)
        return 0

    lax.fori_loop(0, 4, turn, 0)

    pltpu.make_async_copy(out, out, p_recv).wait()

    def sent(k, _):
        pltpu.make_async_copy(pack.at[0, 0], pack.at[0, 0], p_send).wait()
        return 0

    lax.fori_loop(0, 31, sent, 0)

    for q in range(4):
        @pl.when(t == 0)
        def _():
            for copy in z_copies(q, 7 if q < 2 else 6, mid0, z_recv.at[0])[0]:
                copy.wait_send()

        @pl.when(t == 1)
        def _():
            for copy in z_copies(q, 6, mid1, z_recv.at[1])[0]:
                copy.wait_send()


def corner_turn(samples, table, window, perm):
    dma = pltpu.SemaphoreType.DMA
    hbm = pl.BlockSpec(memory_space=pltpu.HBM)
    return pl.pallas_call(
        turn_kernel,
        out_shape=jax.ShapeDtypeStruct((32, 2, 48, 128), BF16),
        in_specs=[hbm, hbm, hbm, hbm],
        out_specs=pl.BlockSpec(memory_space=pl.ANY),
        scratch_shapes=[
            pltpu.VMEM((6, 64, FRAME), BF16),
            pltpu.VMEM((4, 256, FRAME), BF16),
            pltpu.VMEM((TAPS, FRAME), F32),
            pltpu.VMEM((384, 384), BF16),
            pltpu.VMEM((LANE_TILES, 80, 128), F32),
            pltpu.VMEM((6, 8, FRAME), F32),
            pltpu.VMEM((512, FRAME), BF16),
            pltpu.VMEM((128, 128), F32),
            pltpu.VMEM((4, 7, 128, 128), BF16),
            pltpu.VMEM((4, 4, 7, 16, 128), BF16),
            pltpu.VMEM((4, 4, 6, 16, 128), BF16),
            pltpu.VMEM((4, 8, 2, 48, 128), BF16),
            dma((6,)), dma((4,)), dma((2,)), dma((4,)), dma((2, 4)), dma, dma,
        ],
        compiler_params=pltpu.CompilerParams(
            collective_id=1, has_side_effects=True, vmem_limit_bytes=48 << 20
        ),
        name="corner_turn",
    )(*(pltpu.with_memory_space_constraint(a, pltpu.HBM) for a in (samples, table, window, perm)))


def correlate_kernel(turned, perm, out, left, swapped, vis, sem):
    copies = []
    low = (lax.broadcasted_iota(jnp.int32, (192, 256), 1) % 128) < 64
    for ch in range(2):
        for o in range(4):
            halves = [jnp.concatenate([turned[8 * o + k, h] for k in range(8)], 0) for h in range(2)]
            rows = jnp.dot(
                perm[ch * 192 : (ch + 1) * 192], jnp.concatenate(halves, 1), preferred_element_type=F32
            )
            other = jnp.concatenate([pltpu.roll(rows[:, h * 128 : (h + 1) * 128], 64, 1) for h in range(2)], 1)
            other = jnp.where(low, other, -other).astype(BF16)
            rows = rows.astype(BF16)
            for a in range(4):
                src = slice(a * 48, (a + 1) * 48)
                dst = slice(a * 192 + o * 48, a * 192 + (o + 1) * 48)
                left[ch, dst] = rows[src]
                swapped[ch, dst] = other[src]
        for part, mat in enumerate((left, swapped)):
            for r in range(3):
                block = slice(r * 256, (r + 1) * 256)
                vis[ch, part, block] = lax.dot_general(
                    mat[ch, block], left[ch], NT, preferred_element_type=F32
                ) * (1.0 / 128.0)
                copy = pltpu.make_async_copy(
                    vis.at[ch, part, pl.ds(r * 256, 256)],
                    out.at[ch, part, pl.ds(r * 256, 256)],
                    sem.at[ch, part, r],
                )
                copy.start()
                copies.append(copy)
    for copy in copies:
        copy.wait()


def correlate(turned, perm):
    vmem = pl.BlockSpec(memory_space=pltpu.VMEM)
    return pl.pallas_call(
        correlate_kernel,
        out_shape=jax.ShapeDtypeStruct((2, 2, 768, 768), F32),
        in_specs=[vmem, vmem],
        out_specs=pl.BlockSpec(memory_space=pl.ANY),
        scratch_shapes=[
            pltpu.VMEM((2, 768, 256), BF16),
            pltpu.VMEM((2, 768, 256), BF16),
            pltpu.VMEM((2, 2, 768, 768), F32),
            pltpu.SemaphoreType.DMA((2, 2, 3)),
        ],
        compiler_params=pltpu.CompilerParams(vmem_limit_bytes=48 << 20),
        name="correlate",
    )(turned, perm)


def local(samples):
    turned = corner_turn(
        samples, jnp.asarray(dft_rows()), jnp.asarray(pfb_weights()), jnp.asarray(middle_shuffle())
    )
    return correlate(turned, jnp.asarray(final_shuffle()))


def solution(mesh):
    return jax.shard_map(
        local,
        mesh=mesh,
        in_specs=(P("inp", "tm", None),),
        out_specs=P(("inp", "tm"), None, None, None),
        check_vma=False,
    )
```

```python
import numpy as np
import jax
import jax.numpy as jnp
import ml_dtypes
from jax import lax
from jax.experimental import pallas as pl
from jax.experimental.pallas import tpu as pltpu
from jax.sharding import PartitionSpec as P

FRAME = 3072
TAPS = 4
CH = 512
FIRST = 256
MESH = pl.DeviceIdType.MESH
F32 = jnp.float32
BF16 = jnp.bfloat16
LANE_TILES = FRAME // 128
HOPS = (2, 1, 3, 0)
RING = (4, 3, 5, 2, 6, 1, 7)
NT = (((1,), (1,)), ((), ()))


def pfb_weights():
    total = TAPS * FRAME
    place = np.arange(total, dtype=np.float64)
    centred = (place - (total - 1) / 2.0) / FRAME
    taper = 0.5 - 0.5 * np.cos(2.0 * np.pi * (place + 0.5) / total)
    vals = np.sinc(centred) * taper
    return (vals / np.sqrt(np.sum(vals * vals) / FRAME)).reshape(TAPS, FRAME).astype(np.float32)


def dft_rows():
    xd, zd, yd, cd, ch2 = np.meshgrid(
        np.arange(4), np.arange(8), np.arange(4), np.arange(2), np.arange(2), indexing="ij"
    )
    chan = (zd % 4) * 128 + xd * 32 + yd * 8 + cd * 4 + (zd // 4) * 2 + ch2
    chan = chan.reshape(4, 128)
    phase = ((chan[:, :, None] + FIRST) * np.arange(FRAME)[None, None, :]) % FRAME
    angle = 2.0 * np.pi * np.arange(FRAME) / FRAME
    scale = np.sqrt(2.0 / FRAME)
    cos = (np.cos(angle) * scale).astype(ml_dtypes.bfloat16)
    sin = (-np.sin(angle) * scale).astype(ml_dtypes.bfloat16)
    return np.concatenate([cos[phase], sin[phase]], axis=1)


def shuffle(source):
    n = source.size
    out = np.zeros((n, n), ml_dtypes.bfloat16)
    out[np.arange(n), source.reshape(-1)] = 1.0
    return out


def middle_shuffle():
    place = np.arange(384).reshape(4, 6, 8, 2)
    return shuffle(place.transpose(2, 3, 0, 1))


def final_shuffle():
    place = np.arange(384).reshape(8, 2, 4, 6)
    return shuffle(place.transpose(1, 2, 0, 3))


def turn_kernel(
    samples, table, window_hbm, perm_hbm, out,
    xs, tabs, window, perm, stage, tail, filt, extras, send, mid0, mid1, pack,
    x_sem, t_sem, w_sem, z_send, z_recv, p_send, p_recv,
):
    inp = lax.axis_index("inp")
    t = lax.axis_index("tm")
    zl = inp // 32
    xyc = inp - zl * 32
    x = xyc // 8
    yc = xyc - x * 8
    y = yc // 2
    core = yc - y * 2
    z = t * 4 + zl

    def wrap(value, size):
        return jnp.where(value >= size, value - size, value)

    xs_there = [wrap(x + k, 4) for k in range(4)]
    ycs_there = [2 * wrap(y + k, 4) + c for k in range(4) for c in (core, 1 - core)]

    def chunk_x(q):
        there = xs_there[HOPS[3]]
        for k in range(3):
            there = jnp.where(q == k, xs_there[HOPS[k]], there)
        return there

    def z_device(place):
        half = jnp.where(place >= 4, 1, 0)
        return ((place - half * 4) * 32 + xyc, half)

    def p_device(xd, there):
        return (zl * 32 + xd * 8 + there, t)

    barrier = pltpu.get_barrier_semaphore()
    for k in RING:
        pl.semaphore_signal(barrier, inc=1, device_id=z_device(wrap(z + k, 8)), device_id_type=MESH)

    def fetch_table(q):
        pltpu.make_async_copy(table.at[chunk_x(q)], tabs.at[q], t_sem.at[q]).start()

    for i in range(2):
        pltpu.make_async_copy(samples.at[i], xs.at[i], x_sem.at[i]).start()
    pltpu.make_async_copy(window_hbm, window, w_sem.at[0]).start()
    fetch_table(0)
    for i in range(2, 6):
        pltpu.make_async_copy(samples.at[i], xs.at[i], x_sem.at[i]).start()

    for k in HOPS:
        for n, there in enumerate(ycs_there):
            if k or n:
                pl.semaphore_signal(
                    barrier, inc=1, device_id=p_device(xs_there[k], there), device_id_type=MESH
                )

    stage[:, 0:8, :] = jnp.zeros((LANE_TILES, 8, 128), F32)
    stage[:, 72:80, :] = jnp.zeros((LANE_TILES, 8, 128), F32)

    pltpu.make_async_copy(window_hbm, window, w_sem.at[0]).wait()

    def filter_input(i, _):
        pltpu.make_async_copy(samples.at[i], xs.at[i], x_sem.at[i]).wait()
        for c in range(LANE_TILES):
            stage[c, 8:72, :] = xs[i, :, c * 128 : (c + 1) * 128].astype(F32)
        for c in range(LANE_TILES):
            cols = slice(c * 128, (c + 1) * 128)
            acc = window[0:1, cols] * stage[c, 5:77, :]
            for k in range(1, TAPS):
                acc = acc + window[k : k + 1, cols] * stage[c, 5 + k : 77 + k, :]
            filt[pl.ds(pl.multiple_of(i * 64, 64), 64), cols] = acc[0:64].astype(BF16)
            tail[i, :, cols] = acc[64:72]
        return 0

    def z_copies(q, first, blocks, mid, sem):
        copies = []
        span = pl.ds(first, blocks)
        for k in RING:
            place = wrap(z + k, 8)
            rows = pl.ds(pl.multiple_of(place * 16, 16), 16)
            copies.append(
                pltpu.make_async_remote_copy(
                    send.at[q, span, rows, :], mid.at[q, zl, span], z_send.at[q], sem.at[q],
                    device_id=z_device(place), device_id_type=MESH,
                )
            )
        rows = pl.ds(pl.multiple_of(z * 16, 16), 16)
        own = pltpu.make_async_copy(send.at[q, span, rows, :], mid.at[q, zl, span], sem.at[q])
        return copies, own

    def send_z(q, first, blocks, mid, sem):
        copies, own = z_copies(q, first, blocks, mid, sem)
        for copy in copies:
            copy.start()
        own.start()

    low = lax.broadcasted_iota(jnp.int32, (128, 128), 1) < 64

    def spread(prod):
        re, im = prod[0:128], prod[128:256]
        even = jnp.where(low, re, pltpu.roll(im, 64, 1)).astype(BF16)
        odd = jnp.where(low, pltpu.roll(re, 64, 1), im).astype(BF16)
        return even, odd

    def put_pair(q, pair, prod):
        even, odd = spread(prod)
        send[q, 2 * pair] = even
        send[q, 2 * pair + 1] = odd

    def begin(pair, _):
        lax.fori_loop(2 * pair, 2 * pair + 2, filter_input, 0)

        @pl.when(pair == 0)
        def _():
            for q in range(1, 4):
                fetch_table(q)
            pltpu.make_async_copy(perm_hbm, perm, w_sem.at[1]).start()
            pltpu.make_async_copy(table.at[0], tabs.at[0], t_sem.at[0]).wait()

        @pl.when(t == 1)
        def _():
            rows = filt[pl.ds(pl.multiple_of(pair * 128, 128), 128), :]
            put_pair(0, pair, lax.dot_general(tabs[0], rows, NT, preferred_element_type=F32))

            @pl.when(pair == 0)
            def _():
                pl.semaphore_wait(barrier, 38)

            send_z(0, 2 * pair, 2, mid1, z_recv.at[1])

        return 0

    lax.fori_loop(0, 3, begin, 0)

    @pl.when(t == 1)
    def _():
        def spectra(q, _):
            pltpu.make_async_copy(table.at[0], tabs.at[q], t_sem.at[q]).wait()
            prod = lax.dot_general(tabs[q], filt[0:384], NT, preferred_element_type=F32)
            for pair in range(3):
                put_pair(q, pair, prod[:, pair * 128 : (pair + 1) * 128])
            send_z(q, 0, 6, mid1, z_recv.at[1])
            return 0

        lax.fori_loop(1, 4, spectra, 0)

    @pl.when(t == 0)
    def _():
        reach = [tail[i, 0 : TAPS - 1, :] for i in range(6)]
        filt[384:416, :] = jnp.concatenate(reach + [jnp.zeros((14, FRAME), F32)], 0).astype(BF16)
        filt[416:512, :] = jnp.zeros((96, FRAME), BF16)

        def spectra(q, _):
            @pl.when(q > 0)
            def _():
                pltpu.make_async_copy(table.at[0], tabs.at[q], t_sem.at[q]).wait()

            prod = lax.dot_general(tabs[q], filt[...], NT, preferred_element_type=F32)
            for pair in range(3):
                put_pair(q, pair, prod[:, pair * 128 : (pair + 1) * 128])
            re, im = prod[0:128, 384:512], prod[128:256, 384:512]

            @pl.when(q == 0)
            def _():
                send[0, 6] = (re + pltpu.roll(im, 20, 1)).astype(BF16)
                extras[...] = jnp.zeros((128, 128), F32)
                pl.semaphore_wait(barrier, 38)
                send_z(0, 0, 7, mid0, z_recv.at[0])

            @pl.when(q > 0)
            def _():
                slot = (q - 1) * 40
                extras[...] += pltpu.roll(re, slot, 1) + pltpu.roll(im, slot + 20, 1)

            return 0

        lax.fori_loop(0, 4, spectra, 0)
        send[1, 6] = extras[...].astype(BF16)
        send_z(1, 0, 7, mid0, z_recv.at[0])
        for q in range(2, 4):
            send_z(q, 0, 6, mid0, z_recv.at[0])

    lane = lax.broadcasted_iota(jnp.int32, (16, 128), 1)
    first = lane < TAPS - 1
    second = (lane >= 64) & (lane < 64 + TAPS - 1)
    pltpu.make_async_copy(perm_hbm, perm, w_sem.at[1]).wait()

    def turn(q, _):
        @pl.when(q < 2)
        def _():
            pltpu.make_async_copy(mid0.at[q], mid0.at[q], z_recv.at[0, q]).wait()

        @pl.when(q >= 2)
        def _():
            pltpu.make_async_copy(mid1.at[q], mid1.at[q], z_recv.at[0, q]).wait()

        pltpu.make_async_copy(mid1.at[q], mid1.at[q], z_recv.at[1, q]).wait()
        later = []
        slot = jnp.maximum(q - 1, 0) * 40
        for a in range(4):
            extra = mid0[jnp.minimum(q, 1), a, 6].astype(F32)
            for i in range(6):
                re = pltpu.roll(extra, (128 - 3 * i - slot) % 128, 1)
                im = pltpu.roll(extra, (172 - 3 * i - slot) % 128, 1)
                added = jnp.where(first, re, jnp.where(second, im, 0.0))
                later.append((mid1[q, a, i].astype(F32) + added).astype(BF16))
        earlier = [mid0[q, a, i] for a in range(4) for i in range(6)]
        both = jnp.concatenate([jnp.concatenate(earlier, 0), jnp.concatenate(later, 0)], 1)
        turned = jnp.dot(perm[...], both, preferred_element_type=F32).astype(BF16)
        for n in range(8):
            for half in range(2):
                pack[q, n, half] = turned[n * 48 : (n + 1) * 48, half * 128 : (half + 1) * 128]
        xd = chunk_x(q)

        def pass_on(there):
            pltpu.make_async_remote_copy(
                pack.at[q, there], out.at[xyc], p_send, p_recv, device_id=p_device(xd, there), device_id_type=MESH
            ).start()

        for n in (4, 5, 2, 3, 6, 7, 1):
            pass_on(ycs_there[n])

        @pl.when(q < 3)
        def _():
            pass_on(yc)

        @pl.when(q == 3)
        def _():
            pltpu.make_async_copy(pack.at[q, yc], out.at[xyc], p_recv).start()

        return 0

    lax.fori_loop(0, 4, turn, 0)

    pltpu.make_async_copy(out, out, p_recv).wait()

    def sent(k, _):
        pltpu.make_async_copy(pack.at[0, 0], pack.at[0, 0], p_send).wait()
        return 0

    lax.fori_loop(0, 31, sent, 0)

    for q in range(4):
        @pl.when(t == 0)
        def _():
            for copy in z_copies(q, 0, 7 if q < 2 else 6, mid0, z_recv.at[0])[0]:
                copy.wait_send()

        @pl.when(t == 1)
        def _():
            for copy in z_copies(q, 0, 6, mid1, z_recv.at[1])[0]:
                copy.wait_send()


def corner_turn(samples, table, window, perm):
    dma = pltpu.SemaphoreType.DMA
    hbm = pl.BlockSpec(memory_space=pltpu.HBM)
    return pl.pallas_call(
        turn_kernel,
        out_shape=jax.ShapeDtypeStruct((32, 2, 48, 128), BF16),
        in_specs=[hbm, hbm, hbm, hbm],
        out_specs=pl.BlockSpec(memory_space=pl.ANY),
        scratch_shapes=[
            pltpu.VMEM((6, 64, FRAME), BF16),
            pltpu.VMEM((4, 256, FRAME), BF16),
            pltpu.VMEM((TAPS, FRAME), F32),
            pltpu.VMEM((384, 384), BF16),
            pltpu.VMEM((LANE_TILES, 80, 128), F32),
            pltpu.VMEM((6, 8, FRAME), F32),
            pltpu.VMEM((512, FRAME), BF16),
            pltpu.VMEM((128, 128), F32),
            pltpu.VMEM((4, 7, 128, 128), BF16),
            pltpu.VMEM((4, 4, 7, 16, 128), BF16),
            pltpu.VMEM((4, 4, 6, 16, 128), BF16),
            pltpu.VMEM((4, 8, 2, 48, 128), BF16),
            dma((6,)), dma((4,)), dma((2,)), dma((4,)), dma((2, 4)), dma, dma,
        ],
        compiler_params=pltpu.CompilerParams(
            collective_id=1, has_side_effects=True, vmem_limit_bytes=48 << 20
        ),
        name="corner_turn",
    )(*(pltpu.with_memory_space_constraint(a, pltpu.HBM) for a in (samples, table, window, perm)))


def correlate_kernel(turned, perm, out, left, swapped, vis, sem):
    copies = []
    low = (lax.broadcasted_iota(jnp.int32, (192, 256), 1) % 128) < 64
    for ch in range(2):
        for o in range(4):
            halves = [jnp.concatenate([turned[8 * o + k, h] for k in range(8)], 0) for h in range(2)]
            rows = jnp.dot(
                perm[ch * 192 : (ch + 1) * 192], jnp.concatenate(halves, 1), preferred_element_type=F32
            )
            other = jnp.concatenate([pltpu.roll(rows[:, h * 128 : (h + 1) * 128], 64, 1) for h in range(2)], 1)
            other = jnp.where(low, other, -other).astype(BF16)
            rows = rows.astype(BF16)
            for a in range(4):
                src = slice(a * 48, (a + 1) * 48)
                dst = slice(a * 192 + o * 48, a * 192 + (o + 1) * 48)
                left[ch, dst] = rows[src]
                swapped[ch, dst] = other[src]
        for part, mat in enumerate((left, swapped)):
            for r in range(3):
                block = slice(r * 256, (r + 1) * 256)
                vis[ch, part, block] = lax.dot_general(
                    mat[ch, block], left[ch], NT, preferred_element_type=F32
                ) * (1.0 / 128.0)
                copy = pltpu.make_async_copy(
                    vis.at[ch, part, pl.ds(r * 256, 256)],
                    out.at[ch, part, pl.ds(r * 256, 256)],
                    sem.at[ch, part, r],
                )
                copy.start()
                copies.append(copy)
    for copy in copies:
        copy.wait()


def correlate(turned, perm):
    vmem = pl.BlockSpec(memory_space=pltpu.VMEM)
    return pl.pallas_call(
        correlate_kernel,
        out_shape=jax.ShapeDtypeStruct((2, 2, 768, 768), F32),
        in_specs=[vmem, vmem],
        out_specs=pl.BlockSpec(memory_space=pl.ANY),
        scratch_shapes=[
            pltpu.VMEM((2, 768, 256), BF16),
            pltpu.VMEM((2, 768, 256), BF16),
            pltpu.VMEM((2, 2, 768, 768), F32),
            pltpu.SemaphoreType.DMA((2, 2, 3)),
        ],
        compiler_params=pltpu.CompilerParams(vmem_limit_bytes=48 << 20),
        name="correlate",
    )(turned, perm)


def local(samples):
    turned = corner_turn(
        samples, jnp.asarray(dft_rows()), jnp.asarray(pfb_weights()), jnp.asarray(middle_shuffle())
    )
    return correlate(turned, jnp.asarray(final_shuffle()))


def solution(mesh):
    return jax.shard_map(
        local,
        mesh=mesh,
        in_specs=(P("inp", "tm", None),),
        out_specs=P(("inp", "tm"), None, None, None),
        check_vma=False,
    )
```

```python
import numpy as np
import jax
import jax.numpy as jnp
import ml_dtypes
from jax import lax
from jax.experimental import pallas as pl
from jax.experimental.pallas import tpu as pltpu
from jax.sharding import PartitionSpec as P

FRAME = 3072
TAPS = 4
CH = 512
FIRST = 256
MESH = pl.DeviceIdType.MESH
F32 = jnp.float32
BF16 = jnp.bfloat16
LANE_TILES = FRAME // 128
GROUPS = (
    ((2, 2), (1, 2), (3, 2), (2, 1)),
    ((2, 3), (0, 2), (1, 1), (3, 3)),
    ((2, 0), (1, 3), (3, 1), (3, 0)),
    ((0, 1), (0, 3), (1, 0), (0, 0)),
)
RING = (4, 3, 5, 2, 6, 1, 7)
NT = (((1,), (1,)), ((), ()))


def pfb_weights():
    total = TAPS * FRAME
    place = np.arange(total, dtype=np.float64)
    centred = (place - (total - 1) / 2.0) / FRAME
    taper = 0.5 - 0.5 * np.cos(2.0 * np.pi * (place + 0.5) / total)
    vals = np.sinc(centred) * taper
    return (vals / np.sqrt(np.sum(vals * vals) / FRAME)).reshape(TAPS, FRAME).astype(np.float32)


def dft_rows():
    xd, yd, zd, cd, ch2 = np.meshgrid(
        np.arange(4), np.arange(4), np.arange(8), np.arange(2), np.arange(2), indexing="ij"
    )
    chan = (zd % 4) * 128 + xd * 32 + yd * 8 + cd * 4 + (zd // 4) * 2 + ch2
    chan = chan.reshape(16, 32)
    phase = ((chan[:, :, None] + FIRST) * np.arange(FRAME)[None, None, :]) % FRAME
    angle = 2.0 * np.pi * np.arange(FRAME) / FRAME
    scale = np.sqrt(2.0 / FRAME)
    cos = (np.cos(angle) * scale).astype(ml_dtypes.bfloat16)
    sin = (-np.sin(angle) * scale).astype(ml_dtypes.bfloat16)
    return np.concatenate([cos[phase], sin[phase]], axis=1)


def shuffle(source):
    n = source.size
    out = np.zeros((n, n), ml_dtypes.bfloat16)
    out[np.arange(n), source.reshape(-1)] = 1.0
    return out


def source_shuffle():
    place = np.arange(128).reshape(4, 8, 2, 2)
    return shuffle(place.transpose(1, 0, 2, 3))


def middle_shuffle():
    place = np.arange(384).reshape(4, 6, 8, 2)
    return shuffle(place.transpose(2, 3, 0, 1))


def final_shuffle():
    place = np.arange(384).reshape(8, 2, 4, 6)
    return shuffle(place.transpose(1, 2, 0, 3))


def turn_kernel(
    samples, table, window_hbm, perm_hbm, order_hbm, out,
    xs, tabs, window, perm, order, stage, tail, filt, extras, send, mid0, mid1, pack,
    x_sem, t_sem, w_sem, z_send, z_recv, p_send, p_recv,
):
    inp = lax.axis_index("inp")
    t = lax.axis_index("tm")
    zl = inp // 32
    xyc = inp - zl * 32
    x = xyc // 8
    yc = xyc - x * 8
    y = yc // 2
    core = yc - y * 2
    z = t * 4 + zl

    def wrap(value, size):
        return jnp.where(value >= size, value - size, value)

    xs_there = [wrap(x + k, 4) for k in range(4)]
    ys_there = [wrap(y + k, 4) for k in range(4)]

    def z_device(place):
        half = jnp.where(place >= 4, 1, 0)
        return ((place - half * 4) * 32 + xyc, half)

    def p_device(dx, dy, c):
        return (zl * 32 + xs_there[dx] * 8 + ys_there[dy] * 2 + c, t)

    barrier = pltpu.get_barrier_semaphore()
    for k in RING:
        pl.semaphore_signal(barrier, inc=1, device_id=z_device(wrap(z + k, 8)), device_id_type=MESH)

    def fetch_table(q):
        for k, (dx, dy) in enumerate(GROUPS[q]):
            chip = xs_there[dx] * 4 + ys_there[dy]
            pltpu.make_async_copy(table.at[chip], tabs.at[q, pl.ds(64 * k, 64)], t_sem.at[q]).start()

    for i in range(2):
        pltpu.make_async_copy(samples.at[i], xs.at[i], x_sem.at[i]).start()
    pltpu.make_async_copy(window_hbm, window, w_sem.at[0]).start()
    pltpu.make_async_copy(order_hbm, order, w_sem.at[2]).start()
    fetch_table(0)
    for i in range(2, 6):
        pltpu.make_async_copy(samples.at[i], xs.at[i], x_sem.at[i]).start()

    for group in GROUPS:
        for dx, dy in group:
            for c in (core, 1 - core):
                if dx or dy or c is not core:
                    pl.semaphore_signal(barrier, inc=1, device_id=p_device(dx, dy, c), device_id_type=MESH)

    stage[:, 0:8, :] = jnp.zeros((LANE_TILES, 8, 128), F32)
    stage[:, 72:80, :] = jnp.zeros((LANE_TILES, 8, 128), F32)

    pltpu.make_async_copy(window_hbm, window, w_sem.at[0]).wait()
    pltpu.make_async_copy(order_hbm, order, w_sem.at[2]).wait()

    def filter_input(i, _):
        pltpu.make_async_copy(samples.at[i], xs.at[i], x_sem.at[i]).wait()
        for c in range(LANE_TILES):
            stage[c, 8:72, :] = xs[i, :, c * 128 : (c + 1) * 128].astype(F32)
        for c in range(LANE_TILES):
            cols = slice(c * 128, (c + 1) * 128)
            acc = window[0:1, cols] * stage[c, 5:77, :]
            for k in range(1, TAPS):
                acc = acc + window[k : k + 1, cols] * stage[c, 5 + k : 77 + k, :]
            filt[pl.ds(pl.multiple_of(i * 64, 64), 64), cols] = acc[0:64].astype(BF16)
            tail[i, :, cols] = acc[64:72]
        return 0

    def z_copies(q, first, blocks, mid, sem):
        copies = []
        span = pl.ds(first, blocks)
        for k in RING:
            place = wrap(z + k, 8)
            copies.append(
                pltpu.make_async_remote_copy(
                    send.at[q, place, span], mid.at[q, zl, span], z_send.at[q], sem.at[q],
                    device_id=z_device(place), device_id_type=MESH,
                )
            )
        own = pltpu.make_async_copy(send.at[q, z, span], mid.at[q, zl, span], sem.at[q])
        return copies, own

    def send_z(q, first, blocks, mid, sem):
        copies, own = z_copies(q, first, blocks, mid, sem)
        for copy in copies:
            copy.start()
        own.start()

    low = lax.broadcasted_iota(jnp.int32, (128, 128), 1) < 64

    def parts(prod):
        re = jnp.concatenate([prod[64 * k : 64 * k + 32] for k in range(4)], 0)
        im = jnp.concatenate([prod[64 * k + 32 : 64 * k + 64] for k in range(4)], 0)
        return re, im

    def put(q, first, prod):
        blocks = []
        for n in range(prod.shape[1] // 128):
            re, im = parts(prod[:, n * 128 : (n + 1) * 128])
            blocks.append(jnp.where(low, re, pltpu.roll(im, 64, 1)).astype(BF16))
            blocks.append(jnp.where(low, pltpu.roll(re, 64, 1), im).astype(BF16))
        moved = jnp.dot(order[...], jnp.concatenate(blocks, 1), preferred_element_type=F32).astype(BF16)
        for n in range(len(blocks)):
            send[q, :, first + n] = moved[:, n * 128 : (n + 1) * 128].reshape(8, 16, 128)

    def put_extras(q, rows):
        moved = jnp.dot(order[...], rows.astype(BF16), preferred_element_type=F32).astype(BF16)
        send[q, :, 6] = moved.reshape(8, 16, 128)

    def begin(pair, _):
        lax.fori_loop(2 * pair, 2 * pair + 2, filter_input, 0)

        @pl.when(pair == 0)
        def _():
            for q in range(1, 4):
                fetch_table(q)
            pltpu.make_async_copy(perm_hbm, perm, w_sem.at[1]).start()
            pltpu.make_async_copy(tabs.at[0], tabs.at[0], t_sem.at[0]).wait()

        @pl.when(t == 1)
        def _():
            rows = filt[pl.ds(pl.multiple_of(pair * 128, 128), 128), :]
            put(0, 2 * pair, lax.dot_general(tabs[0], rows, NT, preferred_element_type=F32))

            @pl.when(pair == 0)
            def _():
                pl.semaphore_wait(barrier, 38)

            send_z(0, 2 * pair, 2, mid1, z_recv.at[1])

        return 0

    lax.fori_loop(0, 3, begin, 0)

    @pl.when(t == 1)
    def _():
        def spectra(q, _):
            pltpu.make_async_copy(tabs.at[q], tabs.at[q], t_sem.at[q]).wait()
            put(q, 0, lax.dot_general(tabs[q], filt[0:384], NT, preferred_element_type=F32))
            send_z(q, 0, 6, mid1, z_recv.at[1])
            return 0

        lax.fori_loop(1, 4, spectra, 0)

    @pl.when(t == 0)
    def _():
        reach = [tail[i, 0 : TAPS - 1, :] for i in range(6)]
        filt[384:416, :] = jnp.concatenate(reach + [jnp.zeros((14, FRAME), F32)], 0).astype(BF16)
        filt[416:512, :] = jnp.zeros((96, FRAME), BF16)

        def spectra(q, _):
            @pl.when(q > 0)
            def _():
                pltpu.make_async_copy(tabs.at[q], tabs.at[q], t_sem.at[q]).wait()

            prod = lax.dot_general(tabs[q], filt[...], NT, preferred_element_type=F32)
            put(q, 0, prod[:, 0:384])
            re, im = parts(prod[:, 384:512])

            @pl.when(q == 0)
            def _():
                put_extras(0, re + pltpu.roll(im, 20, 1))
                extras[...] = jnp.zeros((128, 128), F32)
                pl.semaphore_wait(barrier, 38)
                send_z(0, 0, 7, mid0, z_recv.at[0])

            @pl.when(q > 0)
            def _():
                slot = (q - 1) * 40
                extras[...] += pltpu.roll(re, slot, 1) + pltpu.roll(im, slot + 20, 1)

            return 0

        lax.fori_loop(0, 4, spectra, 0)
        put_extras(1, extras[...])
        send_z(1, 0, 7, mid0, z_recv.at[0])
        for q in range(2, 4):
            send_z(q, 0, 6, mid0, z_recv.at[0])

    lane = lax.broadcasted_iota(jnp.int32, (16, 128), 1)
    first = lane < TAPS - 1
    second = (lane >= 64) & (lane < 64 + TAPS - 1)
    pltpu.make_async_copy(perm_hbm, perm, w_sem.at[1]).wait()

    for q in range(4):
        arrived = mid0 if q < 2 else mid1
        pltpu.make_async_copy(arrived.at[q], arrived.at[q], z_recv.at[0, q]).wait()
        pltpu.make_async_copy(mid1.at[q], mid1.at[q], z_recv.at[1, q]).wait()
        later = []
        slot = max(q - 1, 0) * 40
        for a in range(4):
            extra = mid0[min(q, 1), a, 6].astype(F32)
            for i in range(6):
                re = pltpu.roll(extra, (128 - 3 * i - slot) % 128, 1)
                im = pltpu.roll(extra, (172 - 3 * i - slot) % 128, 1)
                added = jnp.where(first, re, jnp.where(second, im, 0.0))
                later.append((mid1[q, a, i].astype(F32) + added).astype(BF16))
        earlier = [mid0[q, a, i] for a in range(4) for i in range(6)]
        both = jnp.concatenate([jnp.concatenate(earlier, 0), jnp.concatenate(later, 0)], 1)
        turned = jnp.dot(perm[...], both, preferred_element_type=F32).astype(BF16)
        for n in range(8):
            for half in range(2):
                pack[q, n, half] = turned[n * 48 : (n + 1) * 48, half * 128 : (half + 1) * 128]
        for k, (dx, dy) in enumerate(GROUPS[q]):
            for c in (core, 1 - core):
                if dx or dy or c is not core:
                    pltpu.make_async_remote_copy(
                        pack.at[q, 2 * k + c], out.at[xyc], p_send, p_recv,
                        device_id=p_device(dx, dy, c), device_id_type=MESH,
                    ).start()
                else:
                    pltpu.make_async_copy(pack.at[q, 2 * k + c], out.at[xyc], p_recv).start()

    def z_sent(q, blocks):
        gone = send.at[q, pl.ds(0, 7), pl.ds(0, blocks)]
        pltpu.make_async_copy(gone, gone, z_send.at[q]).wait()

    @pl.when(t == 0)
    def _():
        for q in range(4):
            z_sent(q, 7 if q < 2 else 6)

    @pl.when(t == 1)
    def _():
        for q in range(4):
            z_sent(q, 6)

    gone = pack.at[pl.ds(0, 3)]
    pltpu.make_async_copy(gone, gone, p_send).wait()
    gone = pack.at[3, pl.ds(0, 7)]
    pltpu.make_async_copy(gone, gone, p_send).wait()
    pltpu.make_async_copy(out, out, p_recv).wait()


def corner_turn(samples, table, window, perm, order):
    dma = pltpu.SemaphoreType.DMA
    hbm = pl.BlockSpec(memory_space=pltpu.HBM)
    return pl.pallas_call(
        turn_kernel,
        out_shape=jax.ShapeDtypeStruct((32, 2, 48, 128), BF16),
        in_specs=[hbm] * 5,
        out_specs=pl.BlockSpec(memory_space=pl.ANY),
        scratch_shapes=[
            pltpu.VMEM((6, 64, FRAME), BF16),
            pltpu.VMEM((4, 256, FRAME), BF16),
            pltpu.VMEM((TAPS, FRAME), F32),
            pltpu.VMEM((384, 384), BF16),
            pltpu.VMEM((128, 128), BF16),
            pltpu.VMEM((LANE_TILES, 80, 128), F32),
            pltpu.VMEM((6, 8, FRAME), F32),
            pltpu.VMEM((512, FRAME), BF16),
            pltpu.VMEM((128, 128), F32),
            pltpu.VMEM((4, 8, 7, 16, 128), BF16),
            pltpu.VMEM((4, 4, 7, 16, 128), BF16),
            pltpu.VMEM((4, 4, 6, 16, 128), BF16),
            pltpu.VMEM((4, 8, 2, 48, 128), BF16),
            dma((6,)), dma((4,)), dma((3,)), dma((4,)), dma((2, 4)), dma, dma,
        ],
        compiler_params=pltpu.CompilerParams(
            collective_id=1, has_side_effects=True, vmem_limit_bytes=48 << 20
        ),
        name="corner_turn",
    )(*(pltpu.with_memory_space_constraint(a, pltpu.HBM) for a in (samples, table, window, perm, order)))


def correlate_kernel(turned, perm, out, left, swapped, vis, sem):
    copies = []
    low = (lax.broadcasted_iota(jnp.int32, (192, 256), 1) % 128) < 64
    for ch in range(2):
        sorted_rows = []
        for o in range(4):
            halves = [jnp.concatenate([turned[8 * o + k, h] for k in range(8)], 0) for h in range(2)]
            rows = jnp.dot(
                perm[ch * 192 : (ch + 1) * 192], jnp.concatenate(halves, 1), preferred_element_type=F32
            )
            sorted_rows.append(rows)
            for a in range(4):
                left[ch, a * 192 + o * 48 : a * 192 + (o + 1) * 48] = rows[a * 48 : (a + 1) * 48].astype(BF16)
        for part, mat in enumerate((left, swapped)):
            if part:
                for o, rows in enumerate(sorted_rows):
                    other = [pltpu.roll(rows[:, h * 128 : (h + 1) * 128], 64, 1) for h in range(2)]
                    other = jnp.concatenate(other, 1)
                    other = jnp.where(low, other, -other).astype(BF16)
                    for a in range(4):
                        swapped[ch, a * 192 + o * 48 : a * 192 + (o + 1) * 48] = other[a * 48 : (a + 1) * 48]
            for r in range(3):
                block = slice(r * 256, (r + 1) * 256)
                vis[ch, part, block] = lax.dot_general(
                    mat[ch, block], left[ch], NT, preferred_element_type=F32
                ) * (1.0 / 128.0)
                copy = pltpu.make_async_copy(
                    vis.at[ch, part, pl.ds(r * 256, 256)],
                    out.at[ch, part, pl.ds(r * 256, 256)],
                    sem.at[ch, part, r],
                )
                copy.start()
                copies.append(copy)
    for copy in copies:
        copy.wait()


def correlate(turned, perm):
    vmem = pl.BlockSpec(memory_space=pltpu.VMEM)
    return pl.pallas_call(
        correlate_kernel,
        out_shape=jax.ShapeDtypeStruct((2, 2, 768, 768), F32),
        in_specs=[vmem, vmem],
        out_specs=pl.BlockSpec(memory_space=pl.ANY),
        scratch_shapes=[
            pltpu.VMEM((2, 768, 256), BF16),
            pltpu.VMEM((2, 768, 256), BF16),
            pltpu.VMEM((2, 2, 768, 768), F32),
            pltpu.SemaphoreType.DMA((2, 2, 3)),
        ],
        compiler_params=pltpu.CompilerParams(vmem_limit_bytes=48 << 20),
        name="correlate",
    )(turned, perm)


def local(samples):
    turned = corner_turn(
        samples,
        jnp.asarray(dft_rows()),
        jnp.asarray(pfb_weights()),
        jnp.asarray(middle_shuffle()),
        jnp.asarray(source_shuffle()),
    )
    return correlate(turned, jnp.asarray(final_shuffle()))


def solution(mesh):
    return jax.shard_map(
        local,
        mesh=mesh,
        in_specs=(P("inp", "tm", None),),
        out_specs=P(("inp", "tm"), None, None, None),
        check_vma=False,
    )
```

```python
import numpy as np
import jax
import jax.numpy as jnp
import ml_dtypes
from jax import lax
from jax.experimental import pallas as pl
from jax.experimental.pallas import tpu as pltpu
from jax.sharding import PartitionSpec as P

FRAME = 3072
TAPS = 4
CH = 512
FIRST = 256
MESH = pl.DeviceIdType.MESH
F32 = jnp.float32
BF16 = jnp.bfloat16
LANE_TILES = FRAME // 128
GROUPS = (
    ((2, 2), (2, 1), (2, 3), (3, 2)),
    ((1, 2), (2, 0), (1, 3), (3, 1)),
    ((1, 1), (3, 3), (1, 0), (3, 0)),
    ((0, 2), (0, 1), (0, 3), (0, 0)),
)
RING = (4, 3, 5, 2, 6, 1, 7)
NT = (((1,), (1,)), ((), ()))


def pfb_weights():
    total = TAPS * FRAME
    place = np.arange(total, dtype=np.float64)
    centred = (place - (total - 1) / 2.0) / FRAME
    taper = 0.5 - 0.5 * np.cos(2.0 * np.pi * (place + 0.5) / total)
    vals = np.sinc(centred) * taper
    return (vals / np.sqrt(np.sum(vals * vals) / FRAME)).reshape(TAPS, FRAME).astype(np.float32)


def dft_rows():
    xd, yd, zd, cd, ch2 = np.meshgrid(
        np.arange(4), np.arange(4), np.arange(8), np.arange(2), np.arange(2), indexing="ij"
    )
    chan = (zd % 4) * 128 + xd * 32 + yd * 8 + cd * 4 + (zd // 4) * 2 + ch2
    chan = chan.reshape(16, 32)
    phase = ((chan[:, :, None] + FIRST) * np.arange(FRAME)[None, None, :]) % FRAME
    angle = 2.0 * np.pi * np.arange(FRAME) / FRAME
    scale = np.sqrt(2.0 / FRAME)
    cos = (np.cos(angle) * scale).astype(ml_dtypes.bfloat16)
    sin = (-np.sin(angle) * scale).astype(ml_dtypes.bfloat16)
    return np.concatenate([cos[phase], sin[phase]], axis=1)


def shuffle(source, columns=None):
    source = source.reshape(-1)
    out = np.zeros((source.size, columns or source.size), ml_dtypes.bfloat16)
    out[np.arange(source.size), source] = 1.0
    return out


def final_shuffle():
    return shuffle(np.arange(384).reshape(8, 2, 4, 6).transpose(1, 2, 0, 3))


def small_matrices():
    out = np.zeros((192, 640), ml_dtypes.bfloat16)
    out[:, 0:192] = shuffle(np.arange(192).reshape(6, 8, 2, 2).transpose(2, 1, 3, 0))
    out[:128, 256:384] = shuffle(np.arange(128).reshape(4, 8, 2, 2).transpose(1, 0, 2, 3))
    for i in range(6):
        for j in range(TAPS - 1):
            out[80 + 3 * i + j, 384 + j] = 1.0
            out[100 + 3 * i + j, 384 + 64 + j] = 1.0
    for n in range(8):
        for a in range(4):
            for ch in range(2):
                out[n * 16 + a * 2 + ch, 512 + a * 16 + n * 2 + ch] = 1.0
    return out


def large_matrices():
    out = np.zeros((384, 1024), ml_dtypes.bfloat16)
    out[:, 0:384] = shuffle(np.arange(384).reshape(4, 6, 8, 2).transpose(2, 3, 0, 1))
    out[:, 384:768] = shuffle(np.arange(384).reshape(8, 4, 2, 6).transpose(1, 2, 0, 3))
    zl, ch, yc, i = np.meshgrid(np.arange(4), np.arange(2), np.arange(8), np.arange(6), indexing="ij")
    out[:, 768:896] = shuffle(yc * 16 + zl * 2 + ch, 128)
    lane = np.arange(128)[None, :]
    start = 80 + 3 * i.reshape(-1, 1)
    own = (lane >= start) & (lane < start + TAPS - 1)
    own |= (lane >= start + 20) & (lane < start + 20 + TAPS - 1)
    out[:, 896:1024] = own
    return out


def turn_kernel(
    samples, table, window_hbm, large_hbm, small_hbm, out, last, added_out,
    xs, tabs, window, large, small, stage, tail, filt, extras, send, mid0, mid1, pack,
    send3, mid3, pack3, pack_e, mid_e, expanded,
    x_sem, t_sem, w_sem, z_send, z_recv, p_send, p_recv, s_sem, r_sem,
):
    inp = lax.axis_index("inp")
    t = lax.axis_index("tm")
    zl = inp // 32
    xyc = inp - zl * 32
    x = xyc // 8
    yc = xyc - x * 8
    y = yc // 2
    core = yc - y * 2
    z = t * 4 + zl

    def wrap(value, size):
        return jnp.where(value >= size, value - size, value)

    xs_there = [wrap(x + k, 4) for k in range(4)]
    ys_there = [wrap(y + k, 4) for k in range(4)]

    def z_device(place):
        half = jnp.where(place >= 4, 1, 0)
        return ((place - half * 4) * 32 + xyc, half)

    def p_device(dx, dy, c):
        return (zl * 32 + xs_there[dx] * 8 + ys_there[dy] * 2 + c, t)

    z_others = [(1 - t) * 4 + wrap(zl + k, 4) for k in range(4)]
    z_others += [t * 4 + wrap(zl + k, 4) for k in (2, 1, 3)]

    barrier = pltpu.get_barrier_semaphore()
    for k in RING:
        pl.semaphore_signal(barrier, inc=1, device_id=z_device(wrap(z + k, 8)), device_id_type=MESH)

    def fetch_table(q):
        for k, (dx, dy) in enumerate(GROUPS[q]):
            chip = xs_there[dx] * 4 + ys_there[dy]
            pltpu.make_async_copy(table.at[chip], tabs.at[q, pl.ds(64 * k, 64)], t_sem.at[q]).start()

    for i in range(2):
        pltpu.make_async_copy(samples.at[i], xs.at[i], x_sem.at[i]).start()
    pltpu.make_async_copy(window_hbm, window, w_sem.at[0]).start()
    pltpu.make_async_copy(small_hbm, small, w_sem.at[2]).start()
    fetch_table(0)
    for i in range(2, 6):
        pltpu.make_async_copy(samples.at[i], xs.at[i], x_sem.at[i]).start()

    for group in GROUPS:
        for dx, dy in group:
            for c in (core, 1 - core):
                if dx or dy or c is not core:
                    pl.semaphore_signal(barrier, inc=1, device_id=p_device(dx, dy, c), device_id_type=MESH)

    stage[:, 0:8, :] = jnp.zeros((LANE_TILES, 8, 128), F32)
    stage[:, 72:80, :] = jnp.zeros((LANE_TILES, 8, 128), F32)

    pltpu.make_async_copy(window_hbm, window, w_sem.at[0]).wait()
    pltpu.make_async_copy(small_hbm, small, w_sem.at[2]).wait()

    def filter_input(i, _):
        pltpu.make_async_copy(samples.at[i], xs.at[i], x_sem.at[i]).wait()
        for c in range(LANE_TILES):
            stage[c, 8:72, :] = xs[i, :, c * 128 : (c + 1) * 128].astype(F32)
        for c in range(LANE_TILES):
            cols = slice(c * 128, (c + 1) * 128)
            acc = window[0:1, cols] * stage[c, 5:77, :]
            for k in range(1, TAPS):
                acc = acc + window[k : k + 1, cols] * stage[c, 5 + k : 77 + k, :]
            filt[pl.ds(pl.multiple_of(i * 64, 64), 64), cols] = acc[0:64].astype(BF16)
            tail[i, :, cols] = acc[64:72]
        return 0

    def z_copies(q, first, blocks, mid, sem):
        copies = []
        span = pl.ds(first, blocks)
        for place in z_others:
            copies.append(
                pltpu.make_async_remote_copy(
                    send.at[q, place, span], mid.at[q, zl, span], z_send.at[q], sem.at[q],
                    device_id=z_device(place), device_id_type=MESH,
                )
            )
        own = pltpu.make_async_copy(send.at[q, z, span], mid.at[q, zl, span], sem.at[q])
        return copies, own

    def send_z(q, first, blocks, mid, sem):
        copies, own = z_copies(q, first, blocks, mid, sem)
        for copy in copies:
            copy.start()
        own.start()

    low = lax.broadcasted_iota(jnp.int32, (128, 128), 1) < 64

    def parts(prod):
        re = jnp.concatenate([prod[64 * k : 64 * k + 32] for k in range(4)], 0)
        im = jnp.concatenate([prod[64 * k + 32 : 64 * k + 64] for k in range(4)], 0)
        return re, im

    def blocks_of(prod):
        blocks = []
        for n in range(prod.shape[1] // 128):
            re, im = parts(prod[:, n * 128 : (n + 1) * 128])
            blocks.append(jnp.where(low, re, pltpu.roll(im, 64, 1)).astype(BF16))
            blocks.append(jnp.where(low, pltpu.roll(re, 64, 1), im).astype(BF16))
        return blocks

    def put(q, first, prod):
        blocks = blocks_of(prod)
        moved = jnp.dot(small[0:128, 256:384], jnp.concatenate(blocks, 1), preferred_element_type=F32).astype(BF16)
        for n in range(len(blocks)):
            send[q, :, first + n] = moved[:, n * 128 : (n + 1) * 128].reshape(8, 16, 128)

    def to_chips(source, dest, k):
        for n, (dx, dy) in enumerate(GROUPS[3]):
            for c in (core, 1 - core):
                if dy or c is not core:
                    pltpu.make_async_remote_copy(
                        source.at[2 * n + c], dest.at[yc], s_sem.at[k], r_sem.at[k],
                        device_id=p_device(dx, dy, c), device_id_type=MESH,
                    ).start()
                else:
                    pltpu.make_async_copy(source.at[2 * n + c], dest.at[yc], r_sem.at[k]).start()

    def put_last(prod):
        blocks = blocks_of(prod)
        by_chip = [jnp.concatenate([b[32 * k : 32 * k + 32] for b in blocks], 0) for k in range(4)]
        moved = jnp.dot(small[:, 0:192], jnp.concatenate(by_chip, 1), preferred_element_type=F32).astype(BF16)
        for k in range(4):
            for c in range(2):
                send3[2 * k + c] = moved[c * 96 : (c + 1) * 96, k * 128 : (k + 1) * 128]
        to_chips(send3, mid3, 0)

    def put_extras(q, rows):
        moved = jnp.dot(small[0:128, 256:384], rows.astype(BF16), preferred_element_type=F32).astype(BF16)
        send[q, :, 6] = moved.reshape(8, 16, 128)

    def begin(pair, _):
        lax.fori_loop(2 * pair, 2 * pair + 2, filter_input, 0)

        @pl.when(pair == 0)
        def _():
            for q in (3, 1, 2):
                fetch_table(q)
            pltpu.make_async_copy(large_hbm, large, w_sem.at[1]).start()
            pltpu.make_async_copy(tabs.at[0], tabs.at[0], t_sem.at[0]).wait()

        @pl.when(t == 1)
        def _():
            rows = filt[pl.ds(pl.multiple_of(pair * 128, 128), 128), :]
            put(0, 2 * pair, lax.dot_general(tabs[0], rows, NT, preferred_element_type=F32))

            @pl.when(pair == 0)
            def _():
                pl.semaphore_wait(barrier, 38)

            send_z(0, 2 * pair, 2, mid1, z_recv.at[1])

        return 0

    lax.fori_loop(0, 3, begin, 0)

    @pl.when(t == 1)
    def _():
        def product(q):
            pltpu.make_async_copy(tabs.at[q], tabs.at[q], t_sem.at[q]).wait()
            return lax.dot_general(tabs[q], filt[0:384], NT, preferred_element_type=F32)

        put_last(product(3))
        for q in (1, 2):
            put(q, 0, product(q))
            send_z(q, 0, 6, mid1, z_recv.at[1])

    @pl.when(t == 0)
    def _():
        reach = [tail[i, 0 : TAPS - 1, :] for i in range(6)]
        filt[384:416, :] = jnp.concatenate(reach + [jnp.zeros((14, FRAME), F32)], 0).astype(BF16)
        filt[416:512, :] = jnp.zeros((96, FRAME), BF16)

        def product(q):
            if q:
                pltpu.make_async_copy(tabs.at[q], tabs.at[q], t_sem.at[q]).wait()
            return lax.dot_general(tabs[q], filt[...], NT, preferred_element_type=F32)

        prod = product(0)
        put(0, 0, prod[:, 0:384])
        re, im = parts(prod[:, 384:512])
        put_extras(0, re + pltpu.roll(im, 20, 1))
        pl.semaphore_wait(barrier, 38)
        send_z(0, 0, 7, mid0, z_recv.at[0])
        extras[...] = jnp.zeros((128, 128), F32)
        for q in (3, 1, 2):
            prod = product(q)
            if q == 3:
                put_last(prod[:, 0:384])
            else:
                put(q, 0, prod[:, 0:384])
            re, im = parts(prod[:, 384:512])
            slot = (q - 1) * 40
            extras[...] += pltpu.roll(re, slot, 1) + pltpu.roll(im, slot + 20, 1)
        put_extras(1, extras[...])
        send_z(1, 0, 7, mid0, z_recv.at[0])
        send_z(2, 0, 6, mid0, z_recv.at[0])

    lane = lax.broadcasted_iota(jnp.int32, (16, 128), 1)
    first = lane < TAPS - 1
    second = (lane >= 64) & (lane < 64 + TAPS - 1)
    pltpu.make_async_copy(large_hbm, large, w_sem.at[1]).wait()

    for q in range(3):
        def regroup(half, blocks):
            turned = jnp.dot(large[:, 0:384], jnp.concatenate(blocks, 0), preferred_element_type=F32).astype(BF16)
            for n in range(8):
                pack[q, n, half] = turned[n * 48 : (n + 1) * 48]

        arrived = mid0 if q < 2 else mid1
        pltpu.make_async_copy(arrived.at[q], arrived.at[q], z_recv.at[0, q]).wait()
        regroup(0, [mid0[q, a, i] for a in range(4) for i in range(6)])
        slot = max(q - 1, 0) * 40
        added = []
        for a in range(4):
            extra = mid0[min(q, 1), a, 6].astype(F32)
            for i in range(6):
                re = pltpu.roll(extra, (128 - 3 * i - slot) % 128, 1)
                im = pltpu.roll(extra, (172 - 3 * i - slot) % 128, 1)
                added.append(jnp.where(first, re, jnp.where(second, im, 0.0)))
        pltpu.make_async_copy(mid1.at[q], mid1.at[q], z_recv.at[1, q]).wait()
        later = [(mid1[q, n // 6, n % 6].astype(F32) + added[n]).astype(BF16) for n in range(24)]
        regroup(1, later)
        for k, (dx, dy) in enumerate(GROUPS[q]):
            for c in (core, 1 - core):
                pltpu.make_async_remote_copy(
                    pack.at[q, 2 * k + c], out.at[xyc], p_send, p_recv,
                    device_id=p_device(dx, dy, c), device_id_type=MESH,
                ).start()

        if q == 0:
            pltpu.make_async_copy(mid3, mid3, r_sem.at[0]).wait()
            quads = [
                jnp.concatenate([mid3[n, h * 48 : (h + 1) * 48] for n in range(8)], 0) for h in range(2)
            ]
            turned = jnp.dot(large[:, 384:768], jnp.concatenate(quads, 1), preferred_element_type=F32).astype(BF16)
            for h in range(2):
                for a in range(4):
                    pack3[h * 4 + a] = turned[a * 96 : (a + 1) * 96, h * 128 : (h + 1) * 128]
            for place in z_others:
                pltpu.make_async_remote_copy(
                    pack3.at[place], last.at[z], s_sem.at[1], r_sem.at[1],
                    device_id=z_device(place), device_id_type=MESH,
                ).start()
            pltpu.make_async_copy(pack3.at[z], last.at[z], r_sem.at[1]).start()
        if q == 1:
            rows = jnp.concatenate([mid0[1, a, 6] for a in range(4)], 0)
            rows = jnp.dot(small[0:128, 512:576], rows, preferred_element_type=F32).astype(BF16)
            for n in range(8):
                pack_e[n] = rows[n * 16 : (n + 1) * 16]
            to_chips(pack_e, mid_e, 2)

    pltpu.make_async_copy(mid_e, mid_e, r_sem.at[2]).wait()
    rows = jnp.concatenate([mid_e[n] for n in range(8)], 0)
    rows = jnp.dot(large[:, 768:896], rows, preferred_element_type=F32)
    rows = jnp.where(large[:, 896:1024].astype(F32) > 0.5, rows, 0.0).astype(BF16)
    expanded[...] = jnp.dot(rows, small[0:128, 384:512], preferred_element_type=F32).astype(BF16)
    pltpu.make_async_copy(expanded, added_out, w_sem.at[3]).start()

    def all_gone(buffer, sem):
        pltpu.make_async_copy(buffer, buffer, sem).wait()

    @pl.when(t == 0)
    def _():
        for q in range(3):
            all_gone(send.at[q, pl.ds(0, 7), pl.ds(0, 7 if q < 2 else 6)], z_send.at[q])

    @pl.when(t == 1)
    def _():
        for q in range(3):
            all_gone(send.at[q, pl.ds(0, 7), pl.ds(0, 6)], z_send.at[q])

    all_gone(send3.at[pl.ds(0, 7)], s_sem.at[0])
    all_gone(pack_e.at[pl.ds(0, 7)], s_sem.at[2])
    all_gone(pack.at[pl.ds(0, 3)], p_send)
    all_gone(expanded, w_sem.at[3])
    all_gone(out.at[pl.ds(0, 24)], p_recv)
    all_gone(pack3.at[pl.ds(0, 7)], s_sem.at[1])
    all_gone(last, r_sem.at[1])


def corner_turn(samples, table, window, large, small):
    dma = pltpu.SemaphoreType.DMA
    hbm = pl.BlockSpec(memory_space=pltpu.HBM)
    anywhere = pl.BlockSpec(memory_space=pl.ANY)
    operands = (samples, table, window, large, small)
    return pl.pallas_call(
        turn_kernel,
        out_shape=(
            jax.ShapeDtypeStruct((32, 2, 48, 128), BF16),
            jax.ShapeDtypeStruct((8, 96, 128), BF16),
            jax.ShapeDtypeStruct((384, 128), BF16),
        ),
        in_specs=[hbm] * 5,
        out_specs=(anywhere, anywhere, anywhere),
        scratch_shapes=[
            pltpu.VMEM((6, 64, FRAME), BF16),
            pltpu.VMEM((4, 256, FRAME), BF16),
            pltpu.VMEM((TAPS, FRAME), F32),
            pltpu.VMEM((384, 1024), BF16),
            pltpu.VMEM((192, 640), BF16),
            pltpu.VMEM((LANE_TILES, 80, 128), F32),
            pltpu.VMEM((6, 8, FRAME), F32),
            pltpu.VMEM((512, FRAME), BF16),
            pltpu.VMEM((128, 128), F32),
            pltpu.VMEM((3, 8, 7, 16, 128), BF16),
            pltpu.VMEM((3, 4, 7, 16, 128), BF16),
            pltpu.VMEM((3, 4, 6, 16, 128), BF16),
            pltpu.VMEM((3, 8, 2, 48, 128), BF16),
            pltpu.VMEM((8, 96, 128), BF16),
            pltpu.VMEM((8, 96, 128), BF16),
            pltpu.VMEM((8, 96, 128), BF16),
            pltpu.VMEM((8, 16, 128), BF16),
            pltpu.VMEM((8, 16, 128), BF16),
            pltpu.VMEM((384, 128), BF16),
            dma((6,)), dma((4,)), dma((4,)), dma((3,)), dma((2, 3)), dma, dma, dma((3,)), dma((3,)),
        ],
        compiler_params=pltpu.CompilerParams(
            collective_id=1, has_side_effects=True, vmem_limit_bytes=48 << 20
        ),
        name="corner_turn",
    )(*(pltpu.with_memory_space_constraint(a, pltpu.HBM) for a in operands))


def correlate_kernel(turned, last, added, perm, out, left, swapped, vis, sem):
    x = (lax.axis_index("inp") // 8) % 4
    copies = []
    low = (lax.broadcasted_iota(jnp.int32, (768, 128), 1)) < 64
    for ch in range(2):
        for o in range(4):
            halves = [jnp.concatenate([turned[8 * o + k, h] for k in range(8)], 0) for h in range(2)]
            rows = jnp.dot(
                perm[ch * 192 : (ch + 1) * 192], jnp.concatenate(halves, 1), preferred_element_type=F32
            ).astype(BF16)
            for a in range(4):
                left[ch, a * 192 + o * 48 : a * 192 + (o + 1) * 48] = rows[a * 48 : (a + 1) * 48]

        for a in range(4):
            dst = pl.ds(pl.multiple_of(a * 192 + x * 48, 16), 48)
            src = slice(ch * 48, (ch + 1) * 48)
            more = added[(a * 2 + ch) * 48 : (a * 2 + ch + 1) * 48].astype(F32)
            left[ch, dst, 0:128] = last[a, src]
            left[ch, dst, 128:256] = (last[4 + a, src].astype(F32) + more).astype(BF16)
        for part, mat in enumerate((left, swapped)):
            if part:
                for h in range(2):
                    lanes = slice(h * 128, (h + 1) * 128)
                    other = pltpu.roll(left[ch, :, lanes].astype(F32), 64, 1)
                    swapped[ch, :, lanes] = jnp.where(low, other, -other).astype(BF16)
            for r in range(3):
                block = slice(r * 256, (r + 1) * 256)
                vis[ch, part, block] = lax.dot_general(
                    mat[ch, block], left[ch], NT, preferred_element_type=F32
                ) * (1.0 / 128.0)
                copy = pltpu.make_async_copy(
                    vis.at[ch, part, pl.ds(r * 256, 256)],
                    out.at[ch, part, pl.ds(r * 256, 256)],
                    sem.at[ch, part, r],
                )
                copy.start()
                copies.append(copy)
    for copy in copies:
        copy.wait()


def correlate(turned, last, added, perm):
    vmem = pl.BlockSpec(memory_space=pltpu.VMEM)
    return pl.pallas_call(
        correlate_kernel,
        out_shape=jax.ShapeDtypeStruct((2, 2, 768, 768), F32),
        in_specs=[vmem] * 4,
        out_specs=pl.BlockSpec(memory_space=pl.ANY),
        scratch_shapes=[
            pltpu.VMEM((2, 768, 256), BF16),
            pltpu.VMEM((2, 768, 256), BF16),
            pltpu.VMEM((2, 2, 768, 768), F32),
            pltpu.SemaphoreType.DMA((2, 2, 3)),
        ],
        compiler_params=pltpu.CompilerParams(vmem_limit_bytes=48 << 20),
        name="correlate",
    )(turned, last, added, perm)


def local(samples):
    turned, last, added = corner_turn(
        samples,
        jnp.asarray(dft_rows()),
        jnp.asarray(pfb_weights()),
        jnp.asarray(large_matrices()),
        jnp.asarray(small_matrices()),
    )
    return correlate(turned, last, added, jnp.asarray(final_shuffle()))


def solution(mesh):
    return jax.shard_map(
        local,
        mesh=mesh,
        in_specs=(P("inp", "tm", None),),
        out_specs=P(("inp", "tm"), None, None, None),
        check_vma=False,
    )
```

```python
import numpy as np
import jax
import jax.numpy as jnp
import ml_dtypes
from jax import lax
from jax.experimental import pallas as pl
from jax.experimental.pallas import tpu as pltpu
from jax.sharding import PartitionSpec as P

FRAME = 3072
TAPS = 4
CH = 512
FIRST = 256
MESH = pl.DeviceIdType.MESH
F32 = jnp.float32
BF16 = jnp.bfloat16
LANE_TILES = FRAME // 128
GROUPS = (
    ((2, 2), (2, 1), (2, 3), (3, 2)),
    ((1, 2), (2, 0), (1, 3), (3, 1)),
    ((1, 1), (3, 3), (1, 0), (3, 0)),
    ((0, 2), (0, 1), (0, 3), (0, 0)),
)
RING = (4, 3, 5, 2, 6, 1, 7)
NT = (((1,), (1,)), ((), ()))


def pfb_weights():
    total = TAPS * FRAME
    place = np.arange(total, dtype=np.float64)
    centred = (place - (total - 1) / 2.0) / FRAME
    taper = 0.5 - 0.5 * np.cos(2.0 * np.pi * (place + 0.5) / total)
    vals = np.sinc(centred) * taper
    return (vals / np.sqrt(np.sum(vals * vals) / FRAME)).reshape(TAPS, FRAME).astype(np.float32)


def dft_rows():
    xd, yd, zd, cd, ch2 = np.meshgrid(
        np.arange(4), np.arange(4), np.arange(8), np.arange(2), np.arange(2), indexing="ij"
    )
    chan = (zd % 4) * 128 + xd * 32 + yd * 8 + cd * 4 + (zd // 4) * 2 + ch2
    chan = chan.reshape(16, 32)
    phase = ((chan[:, :, None] + FIRST) * np.arange(FRAME)[None, None, :]) % FRAME
    angle = 2.0 * np.pi * np.arange(FRAME) / FRAME
    scale = np.sqrt(2.0 / FRAME)
    cos = (np.cos(angle) * scale).astype(ml_dtypes.bfloat16)
    sin = (-np.sin(angle) * scale).astype(ml_dtypes.bfloat16)
    return np.concatenate([cos[phase], sin[phase]], axis=1)


def shuffle(source, columns=None):
    source = source.reshape(-1)
    out = np.zeros((source.size, columns or source.size), ml_dtypes.bfloat16)
    out[np.arange(source.size), source] = 1.0
    return out


def final_shuffle():
    return shuffle(np.arange(384).reshape(8, 2, 4, 6).transpose(1, 2, 0, 3))


def small_matrices():
    out = np.zeros((192, 640), ml_dtypes.bfloat16)
    out[:, 0:192] = shuffle(np.arange(192).reshape(6, 8, 2, 2).transpose(2, 1, 3, 0))
    out[:128, 256:384] = shuffle(np.arange(128).reshape(4, 8, 2, 2).transpose(1, 0, 2, 3))
    for i in range(6):
        for j in range(TAPS - 1):
            out[80 + 3 * i + j, 384 + j] = 1.0
            out[100 + 3 * i + j, 384 + 64 + j] = 1.0
    for n in range(8):
        for a in range(4):
            for ch in range(2):
                out[n * 16 + a * 2 + ch, 512 + a * 16 + n * 2 + ch] = 1.0
    return out


def large_matrices():
    out = np.zeros((384, 1024), ml_dtypes.bfloat16)
    out[:, 0:384] = shuffle(np.arange(384).reshape(4, 6, 8, 2).transpose(2, 3, 0, 1))
    out[:, 384:768] = shuffle(np.arange(384).reshape(8, 4, 2, 6).transpose(1, 2, 0, 3))
    zl, ch, yc, i = np.meshgrid(np.arange(4), np.arange(2), np.arange(8), np.arange(6), indexing="ij")
    out[:, 768:896] = shuffle(yc * 16 + zl * 2 + ch, 128)
    lane = np.arange(128)[None, :]
    start = 80 + 3 * i.reshape(-1, 1)
    own = (lane >= start) & (lane < start + TAPS - 1)
    own |= (lane >= start + 20) & (lane < start + 20 + TAPS - 1)
    out[:, 896:1024] = own
    return out


def turn_kernel(
    samples, table, window_hbm, large_hbm, small_hbm, out, last, added_out,
    xs, tabs, window, large, small, stage, tail, filt, extras, send, mid0, mid1, pack,
    send3, mid3, pack3, pack_e, mid_e, expanded,
    x_sem, t_sem, w_sem, z_send, z_recv, p_send, p_recv, s_sem, r_sem,
):
    inp = lax.axis_index("inp")
    t = lax.axis_index("tm")
    zl = inp // 32
    xyc = inp - zl * 32
    x = xyc // 8
    yc = xyc - x * 8
    y = yc // 2
    core = yc - y * 2
    z = t * 4 + zl

    def wrap(value, size):
        return jnp.where(value >= size, value - size, value)

    xs_there = [wrap(x + k, 4) for k in range(4)]
    ys_there = [wrap(y + k, 4) for k in range(4)]

    def z_device(place):
        half = jnp.where(place >= 4, 1, 0)
        return ((place - half * 4) * 32 + xyc, half)

    def p_device(dx, dy, c):
        return (zl * 32 + xs_there[dx] * 8 + ys_there[dy] * 2 + c, t)

    z_others = [(1 - t) * 4 + wrap(zl + k, 4) for k in range(4)]
    for spots in zip((3, 2, 1), (3, 0, 2), (0, 3, 1), (0, 1, 2)):
        spot = spots[3]
        for k in range(3):
            spot = jnp.where(zl == k, spots[k], spot)
        z_others.append(t * 4 + spot)

    barrier = pltpu.get_barrier_semaphore()
    for k in RING:
        pl.semaphore_signal(barrier, inc=1, device_id=z_device(wrap(z + k, 8)), device_id_type=MESH)

    def fetch_table(q):
        for k, (dx, dy) in enumerate(GROUPS[q]):
            chip = xs_there[dx] * 4 + ys_there[dy]
            pltpu.make_async_copy(table.at[chip], tabs.at[q, pl.ds(64 * k, 64)], t_sem.at[q]).start()

    for i in range(2):
        pltpu.make_async_copy(samples.at[i], xs.at[i], x_sem.at[i]).start()
    pltpu.make_async_copy(window_hbm, window, w_sem.at[0]).start()
    pltpu.make_async_copy(small_hbm, small, w_sem.at[2]).start()
    fetch_table(0)
    for i in range(2, 6):
        pltpu.make_async_copy(samples.at[i], xs.at[i], x_sem.at[i]).start()

    for group in GROUPS:
        for dx, dy in group:
            for c in (core, 1 - core):
                if dx or dy or c is not core:
                    pl.semaphore_signal(barrier, inc=1, device_id=p_device(dx, dy, c), device_id_type=MESH)

    stage[:, 0:8, :] = jnp.zeros((LANE_TILES, 8, 128), F32)
    stage[:, 72:80, :] = jnp.zeros((LANE_TILES, 8, 128), F32)

    pltpu.make_async_copy(window_hbm, window, w_sem.at[0]).wait()
    pltpu.make_async_copy(small_hbm, small, w_sem.at[2]).wait()

    def filter_input(i, _):
        pltpu.make_async_copy(samples.at[i], xs.at[i], x_sem.at[i]).wait()
        for c in range(LANE_TILES):
            stage[c, 8:72, :] = xs[i, :, c * 128 : (c + 1) * 128].astype(F32)
        for c in range(LANE_TILES):
            cols = slice(c * 128, (c + 1) * 128)
            acc = window[0:1, cols] * stage[c, 5:77, :]
            for k in range(1, TAPS):
                acc = acc + window[k : k + 1, cols] * stage[c, 5 + k : 77 + k, :]
            filt[pl.ds(pl.multiple_of(i * 64, 64), 64), cols] = acc[0:64].astype(BF16)
            tail[i, :, cols] = acc[64:72]
        return 0

    def z_copies(q, first, blocks, mid, sem):
        copies = []
        span = pl.ds(first, blocks)
        for place in z_others:
            copies.append(
                pltpu.make_async_remote_copy(
                    send.at[q, place, span], mid.at[q, zl, span], z_send.at[q], sem.at[q],
                    device_id=z_device(place), device_id_type=MESH,
                )
            )
        own = pltpu.make_async_copy(send.at[q, z, span], mid.at[q, zl, span], sem.at[q])
        return copies, own

    def send_z(q, first, blocks, mid, sem):
        copies, own = z_copies(q, first, blocks, mid, sem)
        for copy in copies:
            copy.start()
        own.start()

    low = lax.broadcasted_iota(jnp.int32, (128, 128), 1) < 64

    def parts(prod):
        re = jnp.concatenate([prod[64 * k : 64 * k + 32] for k in range(4)], 0)
        im = jnp.concatenate([prod[64 * k + 32 : 64 * k + 64] for k in range(4)], 0)
        return re, im

    def blocks_of(prod):
        blocks = []
        for n in range(prod.shape[1] // 128):
            re, im = parts(prod[:, n * 128 : (n + 1) * 128])
            blocks.append(jnp.where(low, re, pltpu.roll(im, 64, 1)).astype(BF16))
            blocks.append(jnp.where(low, pltpu.roll(re, 64, 1), im).astype(BF16))
        return blocks

    def put(q, first, prod):
        blocks = blocks_of(prod)
        moved = jnp.dot(small[0:128, 256:384], jnp.concatenate(blocks, 1), preferred_element_type=F32).astype(BF16)
        for n in range(len(blocks)):
            send[q, :, first + n] = moved[:, n * 128 : (n + 1) * 128].reshape(8, 16, 128)

    def to_chips(source, dest, k):
        for n, (dx, dy) in enumerate(GROUPS[3]):
            for c in (core, 1 - core):
                if dy or c is not core:
                    pltpu.make_async_remote_copy(
                        source.at[2 * n + c], dest.at[yc], s_sem.at[k], r_sem.at[k],
                        device_id=p_device(dx, dy, c), device_id_type=MESH,
                    ).start()
                else:
                    pltpu.make_async_copy(source.at[2 * n + c], dest.at[yc], r_sem.at[k]).start()

    def put_last(prod):
        blocks = blocks_of(prod)
        by_chip = [jnp.concatenate([b[32 * k : 32 * k + 32] for b in blocks], 0) for k in range(4)]
        moved = jnp.dot(small[:, 0:192], jnp.concatenate(by_chip, 1), preferred_element_type=F32).astype(BF16)
        for k in range(4):
            for c in range(2):
                send3[2 * k + c] = moved[c * 96 : (c + 1) * 96, k * 128 : (k + 1) * 128]
        to_chips(send3, mid3, 0)

    def put_extras(q, rows):
        moved = jnp.dot(small[0:128, 256:384], rows.astype(BF16), preferred_element_type=F32).astype(BF16)
        send[q, :, 6] = moved.reshape(8, 16, 128)

    def begin(pair, _):
        lax.fori_loop(2 * pair, 2 * pair + 2, filter_input, 0)

        @pl.when(pair == 0)
        def _():
            for q in (3, 1, 2):
                fetch_table(q)
            pltpu.make_async_copy(large_hbm, large, w_sem.at[1]).start()
            pltpu.make_async_copy(tabs.at[0], tabs.at[0], t_sem.at[0]).wait()

        @pl.when(t == 1)
        def _():
            rows = filt[pl.ds(pl.multiple_of(pair * 128, 128), 128), :]
            put(0, 2 * pair, lax.dot_general(tabs[0], rows, NT, preferred_element_type=F32))

            @pl.when(pair == 0)
            def _():
                pl.semaphore_wait(barrier, 38)

            send_z(0, 2 * pair, 2, mid1, z_recv.at[1])

        return 0

    lax.fori_loop(0, 3, begin, 0)

    @pl.when(t == 1)
    def _():
        def product(q):
            pltpu.make_async_copy(tabs.at[q], tabs.at[q], t_sem.at[q]).wait()
            return lax.dot_general(tabs[q], filt[0:384], NT, preferred_element_type=F32)

        put_last(product(3))
        for q in (1, 2):
            put(q, 0, product(q))
            send_z(q, 0, 6, mid1, z_recv.at[1])

    @pl.when(t == 0)
    def _():
        reach = [tail[i, 0 : TAPS - 1, :] for i in range(6)]
        filt[384:416, :] = jnp.concatenate(reach + [jnp.zeros((14, FRAME), F32)], 0).astype(BF16)
        filt[416:512, :] = jnp.zeros((96, FRAME), BF16)

        def product(q):
            if q:
                pltpu.make_async_copy(tabs.at[q], tabs.at[q], t_sem.at[q]).wait()
            return lax.dot_general(tabs[q], filt[...], NT, preferred_element_type=F32)

        prod = product(0)
        put(0, 0, prod[:, 0:384])
        re, im = parts(prod[:, 384:512])
        put_extras(0, re + pltpu.roll(im, 20, 1))
        pl.semaphore_wait(barrier, 38)
        send_z(0, 0, 7, mid0, z_recv.at[0])
        extras[...] = jnp.zeros((128, 128), F32)
        for q in (3, 1, 2):
            prod = product(q)
            if q == 3:
                put_last(prod[:, 0:384])
            else:
                put(q, 0, prod[:, 0:384])
            re, im = parts(prod[:, 384:512])
            slot = (q - 1) * 40
            extras[...] += pltpu.roll(re, slot, 1) + pltpu.roll(im, slot + 20, 1)
        put_extras(1, extras[...])
        send_z(1, 0, 7, mid0, z_recv.at[0])
        send_z(2, 0, 6, mid0, z_recv.at[0])

    lane = lax.broadcasted_iota(jnp.int32, (16, 128), 1)
    first = lane < TAPS - 1
    second = (lane >= 64) & (lane < 64 + TAPS - 1)
    pltpu.make_async_copy(large_hbm, large, w_sem.at[1]).wait()

    for q in range(3):
        def regroup(half, blocks):
            turned = jnp.dot(large[:, 0:384], jnp.concatenate(blocks, 0), preferred_element_type=F32).astype(BF16)
            for n in range(8):
                pack[q, n, half] = turned[n * 48 : (n + 1) * 48]

        arrived = mid0 if q < 2 else mid1
        pltpu.make_async_copy(arrived.at[q], arrived.at[q], z_recv.at[0, q]).wait()
        regroup(0, [mid0[q, a, i] for a in range(4) for i in range(6)])
        slot = max(q - 1, 0) * 40
        added = []
        for a in range(4):
            extra = mid0[min(q, 1), a, 6].astype(F32)
            for i in range(6):
                re = pltpu.roll(extra, (128 - 3 * i - slot) % 128, 1)
                im = pltpu.roll(extra, (172 - 3 * i - slot) % 128, 1)
                added.append(jnp.where(first, re, jnp.where(second, im, 0.0)))
        pltpu.make_async_copy(mid1.at[q], mid1.at[q], z_recv.at[1, q]).wait()
        later = [(mid1[q, n // 6, n % 6].astype(F32) + added[n]).astype(BF16) for n in range(24)]
        regroup(1, later)
        for k, (dx, dy) in enumerate(GROUPS[q]):
            for c in (core, 1 - core):
                pltpu.make_async_remote_copy(
                    pack.at[q, 2 * k + c], out.at[xyc], p_send, p_recv,
                    device_id=p_device(dx, dy, c), device_id_type=MESH,
                ).start()

        if q == 0:
            pltpu.make_async_copy(mid3, mid3, r_sem.at[0]).wait()
            quads = [
                jnp.concatenate([mid3[n, h * 48 : (h + 1) * 48] for n in range(8)], 0) for h in range(2)
            ]
            turned = jnp.dot(large[:, 384:768], jnp.concatenate(quads, 1), preferred_element_type=F32).astype(BF16)
            for h in range(2):
                for a in range(4):
                    pack3[h * 4 + a] = turned[a * 96 : (a + 1) * 96, h * 128 : (h + 1) * 128]
            for place in z_others:
                pltpu.make_async_remote_copy(
                    pack3.at[place], last.at[z], s_sem.at[1], r_sem.at[1],
                    device_id=z_device(place), device_id_type=MESH,
                ).start()
            pltpu.make_async_copy(pack3.at[z], last.at[z], r_sem.at[1]).start()
        if q == 1:
            rows = jnp.concatenate([mid0[1, a, 6] for a in range(4)], 0)
            rows = jnp.dot(small[0:128, 512:576], rows, preferred_element_type=F32).astype(BF16)
            for n in range(8):
                pack_e[n] = rows[n * 16 : (n + 1) * 16]
            to_chips(pack_e, mid_e, 2)

    pltpu.make_async_copy(mid_e, mid_e, r_sem.at[2]).wait()
    rows = jnp.concatenate([mid_e[n] for n in range(8)], 0)
    rows = jnp.dot(large[:, 768:896], rows, preferred_element_type=F32)
    rows = jnp.where(large[:, 896:1024].astype(F32) > 0.5, rows, 0.0).astype(BF16)
    expanded[...] = jnp.dot(rows, small[0:128, 384:512], preferred_element_type=F32).astype(BF16)
    pltpu.make_async_copy(expanded, added_out, w_sem.at[3]).start()

    def all_gone(buffer, sem):
        pltpu.make_async_copy(buffer, buffer, sem).wait()

    @pl.when(t == 0)
    def _():
        for q in range(3):
            all_gone(send.at[q, pl.ds(0, 7), pl.ds(0, 7 if q < 2 else 6)], z_send.at[q])

    @pl.when(t == 1)
    def _():
        for q in range(3):
            all_gone(send.at[q, pl.ds(0, 7), pl.ds(0, 6)], z_send.at[q])

    all_gone(send3.at[pl.ds(0, 7)], s_sem.at[0])
    all_gone(pack_e.at[pl.ds(0, 7)], s_sem.at[2])
    all_gone(pack.at[pl.ds(0, 3)], p_send)
    all_gone(expanded, w_sem.at[3])
    all_gone(out.at[pl.ds(0, 24)], p_recv)
    all_gone(pack3.at[pl.ds(0, 7)], s_sem.at[1])
    all_gone(last, r_sem.at[1])


def corner_turn(samples, table, window, large, small):
    dma = pltpu.SemaphoreType.DMA
    hbm = pl.BlockSpec(memory_space=pltpu.HBM)
    anywhere = pl.BlockSpec(memory_space=pl.ANY)
    operands = (samples, table, window, large, small)
    return pl.pallas_call(
        turn_kernel,
        out_shape=(
            jax.ShapeDtypeStruct((32, 2, 48, 128), BF16),
            jax.ShapeDtypeStruct((8, 96, 128), BF16),
            jax.ShapeDtypeStruct((384, 128), BF16),
        ),
        in_specs=[hbm] * 5,
        out_specs=(anywhere, anywhere, anywhere),
        scratch_shapes=[
            pltpu.VMEM((6, 64, FRAME), BF16),
            pltpu.VMEM((4, 256, FRAME), BF16),
            pltpu.VMEM((TAPS, FRAME), F32),
            pltpu.VMEM((384, 1024), BF16),
            pltpu.VMEM((192, 640), BF16),
            pltpu.VMEM((LANE_TILES, 80, 128), F32),
            pltpu.VMEM((6, 8, FRAME), F32),
            pltpu.VMEM((512, FRAME), BF16),
            pltpu.VMEM((128, 128), F32),
            pltpu.VMEM((3, 8, 7, 16, 128), BF16),
            pltpu.VMEM((3, 4, 7, 16, 128), BF16),
            pltpu.VMEM((3, 4, 6, 16, 128), BF16),
            pltpu.VMEM((3, 8, 2, 48, 128), BF16),
            pltpu.VMEM((8, 96, 128), BF16),
            pltpu.VMEM((8, 96, 128), BF16),
            pltpu.VMEM((8, 96, 128), BF16),
            pltpu.VMEM((8, 16, 128), BF16),
            pltpu.VMEM((8, 16, 128), BF16),
            pltpu.VMEM((384, 128), BF16),
            dma((6,)), dma((4,)), dma((4,)), dma((3,)), dma((2, 3)), dma, dma, dma((3,)), dma((3,)),
        ],
        compiler_params=pltpu.CompilerParams(
            collective_id=1, has_side_effects=True, vmem_limit_bytes=48 << 20
        ),
        name="corner_turn",
    )(*(pltpu.with_memory_space_constraint(a, pltpu.HBM) for a in operands))


def correlate_kernel(turned, last, added, perm, out, left, swapped, vis, sem):
    x = (lax.axis_index("inp") // 8) % 4
    copies = []
    low = (lax.broadcasted_iota(jnp.int32, (768, 128), 1)) < 64
    for ch in range(2):
        for o in range(4):
            halves = [jnp.concatenate([turned[8 * o + k, h] for k in range(8)], 0) for h in range(2)]
            rows = jnp.dot(
                perm[ch * 192 : (ch + 1) * 192], jnp.concatenate(halves, 1), preferred_element_type=F32
            ).astype(BF16)
            for a in range(4):
                left[ch, a * 192 + o * 48 : a * 192 + (o + 1) * 48] = rows[a * 48 : (a + 1) * 48]

        for a in range(4):
            dst = pl.ds(pl.multiple_of(a * 192 + x * 48, 16), 48)
            src = slice(ch * 48, (ch + 1) * 48)
            more = added[(a * 2 + ch) * 48 : (a * 2 + ch + 1) * 48].astype(F32)
            left[ch, dst, 0:128] = last[a, src]
            left[ch, dst, 128:256] = (last[4 + a, src].astype(F32) + more).astype(BF16)
        for part, mat in enumerate((left, swapped)):
            if part:
                for h in range(2):
                    lanes = slice(h * 128, (h + 1) * 128)
                    other = pltpu.roll(left[ch, :, lanes].astype(F32), 64, 1)
                    swapped[ch, :, lanes] = jnp.where(low, other, -other).astype(BF16)
            for r in range(3):
                block = slice(r * 256, (r + 1) * 256)
                vis[ch, part, block] = lax.dot_general(
                    mat[ch, block], left[ch], NT, preferred_element_type=F32
                ) * (1.0 / 128.0)
                copy = pltpu.make_async_copy(
                    vis.at[ch, part, pl.ds(r * 256, 256)],
                    out.at[ch, part, pl.ds(r * 256, 256)],
                    sem.at[ch, part, r],
                )
                copy.start()
                copies.append(copy)
    for copy in copies:
        copy.wait()


def correlate(turned, last, added, perm):
    vmem = pl.BlockSpec(memory_space=pltpu.VMEM)
    return pl.pallas_call(
        correlate_kernel,
        out_shape=jax.ShapeDtypeStruct((2, 2, 768, 768), F32),
        in_specs=[vmem] * 4,
        out_specs=pl.BlockSpec(memory_space=pl.ANY),
        scratch_shapes=[
            pltpu.VMEM((2, 768, 256), BF16),
            pltpu.VMEM((2, 768, 256), BF16),
            pltpu.VMEM((2, 2, 768, 768), F32),
            pltpu.SemaphoreType.DMA((2, 2, 3)),
        ],
        compiler_params=pltpu.CompilerParams(vmem_limit_bytes=48 << 20),
        name="correlate",
    )(turned, last, added, perm)


def local(samples):
    turned, last, added = corner_turn(
        samples,
        jnp.asarray(dft_rows()),
        jnp.asarray(pfb_weights()),
        jnp.asarray(large_matrices()),
        jnp.asarray(small_matrices()),
    )
    return correlate(turned, last, added, jnp.asarray(final_shuffle()))


def solution(mesh):
    return jax.shard_map(
        local,
        mesh=mesh,
        in_specs=(P("inp", "tm", None),),
        out_specs=P(("inp", "tm"), None, None, None),
        check_vma=False,
    )
```
